128 devices in a mesh: row: 8 (over x_lo, z), col: 16 (over x_hi, y, core).
Axes of the slice: x: 4 (x_hi: 2, x_lo: 2; x = x_hi * 2 + x_lo), y: 4, z: 4, core: 2. Of those that a mesh axis runs over, the one named last changes fastest.
Arguments:
- coarse_in: bfloat16 [256, 128, 512], P(('row', 'col')), may hold values from -6 to 6
- fine_in: bfloat16 [1024, 512, 256], P('row', 'col'), may hold values from -6 to 6
- band_weight: bfloat16 [4, 512, 512], replicated, may hold values from -0.25 to 0.25
- point_weight: bfloat16 [512, 512], replicated, may hold values from -0.25 to 0.25
- proj_weight: bfloat16 [512, 256], replicated, may hold values from -0.25 to 0.25
- conv_weight: bfloat16 [9, 256, 256], replicated, may hold values from -0.125 to 0.125
- out_cot: bfloat16 [1024, 512, 256], P('row', 'col'), may hold values from -6 to 6
Outputs:
- fine_out: bfloat16 [1024, 512, 256], P('row', 'col')
- grad_conv: float32 [9, 256, 256], replicated
- grad_band: float32 [4, 512, 512], replicated
- grad_point: float32 [512, 512], replicated
- grad_proj: float32 [512, 256], replicated
The draws below stay inside these ranges and needn't reach their ends.
All inputs are finite; a program needn't handle non-finite values.
Results may differ from the reference program's by a relative error of at most 0.017.
Values may be sent and summed in bfloat16 or wider, within the bound.
No kernel may reach another device: no remote copies, remote signals or barrier semaphores. Data moves between devices by JAX's collectives and lax.ppermute only.
A program may use at most 128 MiB of HBM per device.

```python
import jax
import jax.numpy as jnp

C = 512
CF = 256
BANDS = 4
TAPS = 9
CLON = 128
CLAT = 256
FLAT = 1024
FLON = 512


def level_of(stream_key, shape, cuts, smallest, high):
    level, own = 1.0, jax.random.fold_in(stream_key, 6)
    for axis_at, shards_of in cuts:
        heights = jnp.exp(jax.random.uniform(jax.random.fold_in(own, axis_at), (shards_of,), jnp.float32, smallest / len(cuts), high / len(cuts)))
        level = level * jnp.repeat(heights, shape[axis_at] // shards_of).reshape([-1 if axis == axis_at else 1 for axis in range(len(shape))])
    return level


def gaussian(stream_key, extent, spread, reach, shards=(), dtype=jnp.bfloat16):
    gain = level_of(stream_key, extent, shards, -0.22, 0.18) if shards else 1.0
    drawn = jax.random.normal(stream_key, extent, jnp.float32) * spread * gain
    return jnp.minimum(jnp.maximum(drawn, -reach), reach).astype(dtype)


def setup_inputs(seed: int = 0) -> dict:
    key_of = jax.random.split(jax.random.key(seed), 8)
    return {
        "coarse_in": gaussian(key_of[0], (CLAT, CLON, C), 1.0, 6.0, ((0, 128),)),
        "fine_in": gaussian(key_of[1], (FLAT, FLON, CF), 1.0, 6.0, ((0, 8), (1, 16))),
        "band_weight": gaussian(key_of[2], (BANDS, C, C), C ** -0.5, 0.25),
        "point_weight": gaussian(key_of[3], (C, C), C ** -0.5, 0.25),
        "proj_weight": gaussian(key_of[4], (C, CF), C ** -0.5, 0.25),
        "conv_weight": gaussian(key_of[5], (TAPS, CF, CF), (9 * CF) ** -0.5, 0.125),
        "out_cot": gaussian(key_of[6], (FLAT, FLON, CF), 1.0, 6.0, ((0, 8), (1, 16))),
    }


def project_rows(field, weight):
    flat = field.reshape(-1, field.shape[-1])
    result = jnp.dot(flat, weight, preferred_element_type=jnp.float32)
    return result.reshape(field.shape[:-1] + (weight.shape[-1],))

def contract_rows(left, right):
    left_flat = left.reshape(-1, left.shape[-1])
    right_flat = right.reshape(-1, right.shape[-1])
    return jnp.dot(left_flat.T, right_flat, preferred_element_type=jnp.float32)

def haar_split(field):
    even_even = field[0::2, 0::2]
    even_odd = field[0::2, 1::2]
    odd_even = field[1::2, 0::2]
    odd_odd = field[1::2, 1::2]
    return jnp.stack([even_even + even_odd + odd_even + odd_odd, even_even - even_odd + odd_even - odd_odd, even_even + even_odd - odd_even - odd_odd, even_even - even_odd - odd_even + odd_odd]) * 0.5

def haar_merge(bands):
    first, second, third, fourth = (bands[0], bands[1], bands[2], bands[3])
    even_even = (first + second + third + fourth) * 0.5
    even_odd = (first - second + third - fourth) * 0.5
    odd_even = (first + second - third - fourth) * 0.5
    odd_odd = (first - second - third + fourth) * 0.5
    height, width, depth = first.shape
    top_row = jnp.stack([even_even, even_odd], axis=2).reshape(height, 2 * width, depth)
    low_row = jnp.stack([odd_even, odd_odd], axis=2).reshape(height, 2 * width, depth)
    return jnp.stack([top_row, low_row], axis=1).reshape(2 * height, 2 * width, depth)

def upsample(field):
    height, width, depth = field.shape
    grown = jnp.broadcast_to(field[:, None, :, None, :], (height, 4, width, 4, depth))
    return grown.reshape(4 * height, 4 * width, depth)

def pad_field(field):
    return jnp.pad(field, ((1, 1), (1, 1), (0, 0)))

def reference(coarse_in, fine_in, band_weight, point_weight, proj_weight, conv_weight, out_cot):
    coarse = coarse_in.astype(jnp.float32)
    subbands = haar_split(coarse).astype(jnp.bfloat16)
    band_mixed = jnp.einsum('shwc,scd->shwd', subbands.astype(jnp.float32), band_weight.astype(jnp.float32))
    pre_act = haar_merge(band_mixed) + project_rows(coarse_in, point_weight)
    coarse_hidden = jax.nn.gelu(pre_act).astype(jnp.bfloat16)
    coarse_out = project_rows(coarse_hidden, proj_weight).astype(jnp.bfloat16)
    conv_in = (fine_in.astype(jnp.float32) + upsample(coarse_out).astype(jnp.float32)).astype(jnp.bfloat16)
    tile_rows, tile_cols = (conv_in.shape[0], conv_in.shape[1])
    padded = pad_field(conv_in)
    grad_pad = pad_field(out_cot)
    total = jnp.zeros((tile_rows, tile_cols, CF), jnp.float32)
    grad_in = jnp.zeros((tile_rows, tile_cols, CF), jnp.float32)
    kernel_parts = []
    for lat_off in range(3):
        for lon_off in range(3):
            weight = conv_weight[3 * lat_off + lon_off]
            window = padded[lat_off:lat_off + tile_rows, lon_off:lon_off + tile_cols]
            total = total + project_rows(window, weight)
            kernel_parts.append(contract_rows(window, out_cot))
            back_window = grad_pad[2 - lat_off:2 - lat_off + tile_rows, 2 - lon_off:2 - lon_off + tile_cols]
            grad_in = grad_in + project_rows(back_window, weight.T)
    fine_out = total.astype(jnp.bfloat16)
    loss_scale = float(FLAT * FLON) ** (-0.5)
    grad_conv = jnp.stack(kernel_parts) * loss_scale
    d_coarse = grad_in.reshape(CLAT, 4, CLON, 4, CF).sum(axis=(1, 3)).astype(jnp.bfloat16)
    grad_proj = contract_rows(coarse_hidden, d_coarse) * loss_scale
    d_hidden = project_rows(d_coarse, proj_weight.T)
    unused, gelu_pull = jax.vjp(jax.nn.gelu, pre_act)
    d_pre = gelu_pull(d_hidden)[0].astype(jnp.bfloat16)
    grad_point = contract_rows(coarse_in, d_pre) * loss_scale
    d_mixed = haar_split(d_pre.astype(jnp.float32)).astype(jnp.bfloat16)
    grad_band = jnp.einsum('shwc,shwd->scd', subbands.astype(jnp.float32), d_mixed.astype(jnp.float32)) * loss_scale
    return (fine_out, grad_conv, grad_band, grad_point, grad_proj)
```

```python
import functools

import jax
import jax.numpy as jnp
import numpy as np
from jax import lax
from jax.experimental import pallas as pl
from jax.experimental.pallas import tpu as pltpu
from jax.sharding import Mesh
from jax.sharding import PartitionSpec as P

BF = jnp.bfloat16
F32 = jnp.float32
ROW = ("xl", "z")
COL = ("xh", "y", "c")
CHIPS = ("xl", "z", "xh", "y")
GRID = (("xl", 2), ("z", 4), ("xh", 2), ("y", 4), ("c", 2))

C, CF, BANDS, TAPS = 512, 256, 4, 9
TR, TC = 128, 32
IR, IC = 32, 8
CELLS = IR * IC
HB = 16
NB = TR // HB
EARLY = 5 * 2 * 256 + 256
LATE = TAPS * 128
PACK = 4096
PEERS = 64
SCALE = float(1024 * 512) ** (-0.5)
VMEM = 56 * 1024 * 1024


def params(n=1):
    return pltpu.CompilerParams(vmem_limit_bytes=VMEM, dimension_semantics=("arbitrary",) * n)


def dot(a, b, dims=((1,), (0,))):
    return lax.dot_general(a, b, (dims, ((), ())), preferred_element_type=F32)


def haar_matrix():
    out = np.zeros((BANDS, IR // 2, IC // 2, IR, IC), np.float32)
    signs = ((1, 1, 1, 1), (1, -1, 1, -1), (1, 1, -1, -1), (1, -1, -1, 1))
    for k in range(BANDS):
        for i in range(IR // 2):
            for j in range(IC // 2):
                for t in range(4):
                    out[k, i, j, 2 * i + t // 2, 2 * j + t % 2] = 0.5 * signs[k][t]
    return out.reshape(CELLS, CELLS)


def cot_kernel(oc, top, bot, left, right, wconv, shifted, dcoarse, win, sums, pooled):
    i = pl.program_id(0)
    r0 = i * HB
    win[1 : HB + 1, 8 : 8 + TC, :] = oc[pl.ds(r0, HB)].astype(F32)
    before = oc[pl.ds(jnp.maximum(r0 - 1, 0), 1)].astype(F32)
    after = oc[pl.ds(jnp.minimum(r0 + HB, TR - 1), 1)].astype(F32)
    win[0:1, 8 : 8 + TC, :] = jnp.where(i == 0, top[...], before)
    win[HB + 1 : HB + 2, 8 : 8 + TC, :] = jnp.where(i == NB - 1, bot[...], after)
    win[:, 7:8, :] = left[pl.ds(r0, HB + 2)]
    win[:, 8 + TC : 9 + TC, :] = right[pl.ds(r0, HB + 2)]
    for b in range(3):
        shifted[0, :, :, b * CF : (b + 1) * CF] = win[:, 9 - b : 9 - b + TC, :].astype(BF)
    for q in range(HB // 4):
        w = [win[4 * q + t] for t in range(6)]
        mid = w[2] + w[3]
        low = w[1] + mid
        high = mid + w[4]
        for a, part in enumerate((high + w[5], low + w[4], w[0] + low)):
            sums[a, q, 0] = part[:, :128]
            sums[a, q, 1] = part[:, 128:]
    for a in range(3):
        for q in range(HB // 4):
            cells = pl.ds(pl.multiple_of((i * (HB // 4) + q) * IC, IC), IC)
            for h in range(2):
                cols = [sums[a, q, h, pl.ds(7 + s, IC, stride=4), :] for s in range(6)]
                mid = cols[2] + cols[3]
                low = cols[1] + mid
                high = mid + cols[4]
                for b, part in enumerate((high + cols[5], low + cols[4], cols[0] + low)):
                    at = (3 * a + b) * CF + 128 * h
                    pooled[cells, at : at + 128] = part

    @pl.when(i == NB - 1)
    def _():
        total = jnp.zeros((CELLS, CF), F32)
        for t in range(TAPS):
            total += dot(pooled[:, t * CF : (t + 1) * CF].astype(BF), wconv[t], ((1,), (1,)))
        dcoarse[...] = total.astype(BF)


def cot_pass(oc, top, bot, left, right, wconv):
    whole = lambda *s: pl.BlockSpec(s, lambda i: (0,) * len(s))
    return pl.pallas_call(
        cot_kernel,
        grid=(NB,),
        in_specs=[
            whole(TR, TC, CF),
            whole(1, TC, CF),
            whole(1, TC, CF),
            whole(TR + 2, 1, CF),
            whole(TR + 2, 1, CF),
            whole(TAPS, CF, CF),
        ],
        out_specs=[
            pl.BlockSpec((1, HB + 2, TC, 3 * CF), lambda i: (i, 0, 0, 0)),
            whole(CELLS, CF),
        ],
        out_shape=[
            jax.ShapeDtypeStruct((NB, HB + 2, TC, 3 * CF), BF),
            jax.ShapeDtypeStruct((CELLS, CF), BF),
        ],
        scratch_shapes=[
            pltpu.VMEM((HB + 2, 48, CF), F32),
            pltpu.VMEM((3, HB // 4, 2, 48, 128), F32),
            pltpu.VMEM((CELLS, TAPS * CF), F32),
        ],
        compiler_params=params(),
        cost_estimate=pl.CostEstimate(flops=400_000_000, bytes_accessed=10_000_000, transcendentals=0),
        name="cotangent_windows",
    )(oc, top, bot, left, right, wconv)


GELU_A = 0.7978845608028654
GELU_B = 0.044715


def coarse_kernel(x, haar, wband, wpoint, wproj, sub, pre, hidden, cout, mixed):
    k = pl.program_id(0)
    part = dot(haar[pl.ds(pl.multiple_of(k * 64, 64), 64), :], x[...]).astype(BF)
    sub[pl.ds(pl.multiple_of(k * 64, 64), 64), :] = part
    mixed[pl.ds(pl.multiple_of(k * 64, 64), 64), :] = dot(part, wband[0])

    @pl.when(k == BANDS - 1)
    def _():
        m = mixed[...]
        hi = m.astype(BF)
        lo = (m - hi.astype(F32)).astype(BF)
        h = haar[...]
        value = dot(h, hi, ((0,), (0,))) + dot(h, lo, ((0,), (0,))) + dot(x[...], wpoint[...])
        pre[...] = value
        act = 0.5 * value * (1.0 + jnp.tanh(GELU_A * (value + GELU_B * (value * value * value))))
        act = act.astype(BF)
        hidden[...] = act
        cout[...] = dot(act, wproj[...]).astype(BF)


def coarse_pass(x, haar, wband, wpoint, wproj):
    whole = lambda *s: pl.BlockSpec(s, lambda i: (0,) * len(s))
    return pl.pallas_call(
        coarse_kernel,
        grid=(BANDS,),
        in_specs=[
            whole(CELLS, C),
            whole(CELLS, CELLS),
            pl.BlockSpec((1, C, C), lambda i: (i, 0, 0)),
            whole(C, C),
            whole(C, CF),
        ],
        out_specs=[whole(CELLS, C), whole(CELLS, C), whole(CELLS, C), whole(CELLS, CF)],
        out_shape=[
            jax.ShapeDtypeStruct((CELLS, C), BF),
            jax.ShapeDtypeStruct((CELLS, C), F32),
            jax.ShapeDtypeStruct((CELLS, C), BF),
            jax.ShapeDtypeStruct((CELLS, CF), BF),
        ],
        scratch_shapes=[pltpu.VMEM((CELLS, C), F32)],
        compiler_params=params(),
        cost_estimate=pl.CostEstimate(flops=500_000_000, bytes_accessed=5_000_000, transcendentals=131072),
        name="coarse_forward",
    )(x, haar, wband, wpoint, wproj)


def grads_kernel(core, x, haar, wproj, sub, pre, hidden, dco, keep, send):
    value = pre[...]
    square = value * value
    th = jnp.tanh(GELU_A * (value + GELU_B * (value * square)))
    slope = 0.5 * (1.0 + th) + 0.5 * value * (1.0 - th * th) * (GELU_A * (1.0 + 3.0 * GELU_B * square))
    d = dco[...]
    dhid = dot(d, wproj[...], ((1,), (1,)))
    dpre = (dhid * slope).astype(BF)
    dmix = dot(haar[...], dpre).astype(BF)
    for out, c in ((keep, core[0]), (send, 1 - core[0])):
        half = pl.ds(pl.multiple_of(c * 256, 256), 256)
        for k in range(5):
            if k < BANDS:
                g = dot(sub[k * 64 : (k + 1) * 64, half], dmix[k * 64 : (k + 1) * 64], ((0,), (0,)))
            else:
                g = dot(x[:, half], dpre, ((0,), (0,)))
            out[k * 512 : k * 512 + 256, :] = g[:, :256].astype(BF)
            out[k * 512 + 256 : k * 512 + 512, :] = g[:, 256:].astype(BF)
        out[2560:2816, :] = dot(hidden[:, half], d, ((0,), (0,))).astype(BF)


def grads_pass(core, x, haar, wproj, sub, pre, hidden, dco):
    vm = pl.BlockSpec(memory_space=pltpu.VMEM)
    return pl.pallas_call(
        grads_kernel,
        in_specs=[pl.BlockSpec(memory_space=pltpu.SMEM)] + [vm] * 7,
        out_specs=[vm, vm],
        out_shape=[jax.ShapeDtypeStruct((EARLY, 256), BF)] * 2,
        compiler_params=pltpu.CompilerParams(vmem_limit_bytes=VMEM),
        cost_estimate=pl.CostEstimate(flops=600_000_000, bytes_accessed=5_000_000, transcendentals=131072),
        name="coarse_gradients",
    )(core, x, haar, wproj, sub, pre, hidden, dco)


def wgrad_kernel(core, fine, cout, shifted, conv_in, keep, send, up, acc):
    i = pl.program_id(0)
    for q in range(HB // 4):
        cell = cout[q * IC : (q + 1) * IC, :].astype(F32)
        for s in range(4):
            up[q, 0, pl.ds(s, IC, stride=4), :] = cell[:, :128]
            up[q, 1, pl.ds(s, IC, stride=4), :] = cell[:, 128:]
        grown = jnp.concatenate([up[q, 0], up[q, 1]], axis=-1)
        for t in range(4):
            conv_in[4 * q + t] = (fine[4 * q + t].astype(F32) + grown).astype(BF)
    left = conv_in[...].reshape(HB * TC, CF).T
    for a in range(3):
        y = shifted[0, 2 - a : 2 - a + HB].reshape(HB * TC, 3 * CF)
        part = dot(left, y)

        @pl.when(i == 0)
        def _():
            acc[a] = part

        @pl.when(i > 0)
        def _():
            acc[a] += part

    @pl.when(i == NB - 1)
    def _():
        for out, c in ((keep, core[0]), (send, 1 - core[0])):
            half = pl.ds(pl.multiple_of(c * 128, 128), 128)
            for t in range(TAPS):
                b = t % 3
                out[t * 128 : (t + 1) * 128, :] = acc[t // 3, half, b * CF : (b + 1) * CF].astype(BF)


def wgrad_pass(core, fine, cout, shifted):
    whole = lambda *s: pl.BlockSpec(s, lambda i: (0,) * len(s))
    return pl.pallas_call(
        wgrad_kernel,
        grid=(NB,),
        in_specs=[
            pl.BlockSpec(memory_space=pltpu.SMEM),
            pl.BlockSpec((HB, TC, CF), lambda i: (i, 0, 0)),
            pl.BlockSpec((HB // 4 * IC, CF), lambda i: (i, 0)),
            pl.BlockSpec((1, HB + 2, TC, 3 * CF), lambda i: (i, 0, 0, 0)),
        ],
        out_specs=[
            pl.BlockSpec((HB, TC, CF), lambda i: (i, 0, 0)),
            whole(LATE, 256),
            whole(LATE, 256),
        ],
        out_shape=[
            jax.ShapeDtypeStruct((TR, TC, CF), BF),
            jax.ShapeDtypeStruct((LATE, 256), BF),
            jax.ShapeDtypeStruct((LATE, 256), BF),
        ],
        scratch_shapes=[pltpu.VMEM((HB // 4, 2, TC, 128), F32), pltpu.VMEM((3, CF, 3 * CF), F32)],
        compiler_params=params(),
        cost_estimate=pl.CostEstimate(flops=5_000_000_000, bytes_accessed=13_000_000, transcendentals=0),
        name="conv_weight_gradient",
    )(core, fine, cout, shifted)


def conv_kernel(ci, top, bot, left, right, wconv, out, win, wide):
    i = pl.program_id(0)
    r0 = i * HB
    win[1 : HB + 1, 8 : 8 + TC, :] = ci[pl.ds(r0, HB)].astype(F32)
    before = ci[pl.ds(jnp.maximum(r0 - 1, 0), 1)].astype(F32)
    after = ci[pl.ds(jnp.minimum(r0 + HB, TR - 1), 1)].astype(F32)
    win[0:1, 8 : 8 + TC, :] = jnp.where(i == 0, top[...], before)
    win[HB + 1 : HB + 2, 8 : 8 + TC, :] = jnp.where(i == NB - 1, bot[...], after)
    win[:, 7:8, :] = left[pl.ds(r0, HB + 2)]
    win[:, 8 + TC : 9 + TC, :] = right[pl.ds(r0, HB + 2)]
    for b in range(3):
        wide[:, :, b * CF : (b + 1) * CF] = win[:, 7 + b : 7 + b + TC, :].astype(BF)
    total = jnp.zeros((HB * TC, CF), F32)
    for a in range(3):
        total += dot(wide[a : a + HB].reshape(HB * TC, 3 * CF), wconv[a])
    out[...] = total.astype(BF).reshape(HB, TC, CF)


def conv_pass(ci, top, bot, left, right, wconv):
    whole = lambda *s: pl.BlockSpec(s, lambda i: (0,) * len(s))
    return pl.pallas_call(
        conv_kernel,
        grid=(NB,),
        in_specs=[
            whole(TR, TC, CF),
            whole(1, TC, CF),
            whole(1, TC, CF),
            whole(TR + 2, 1, CF),
            whole(TR + 2, 1, CF),
            whole(3, 3 * CF, CF),
        ],
        out_specs=pl.BlockSpec((HB, TC, CF), lambda i: (i, 0, 0)),
        out_shape=jax.ShapeDtypeStruct((TR, TC, CF), BF),
        scratch_shapes=[pltpu.VMEM((HB + 2, 48, CF), F32), pltpu.VMEM((HB + 2, TC, 3 * CF), BF)],
        compiler_params=params(),
        cost_estimate=pl.CostEstimate(flops=5_000_000_000, bytes_accessed=6_000_000, transcendentals=0),
        name="conv_forward",
    )(ci, top, bot, left, right, wconv.reshape(3, 3 * CF, CF))


def finish_kernel(core, mine, other, conv, band, point, proj):
    own = core[0] == 0

    def place(out, rows, n, start, cols):
        a = mine[start : start + n, :]
        b = other[start : start + n, :]
        out[rows : rows + n, cols : cols + 256] = jnp.where(own, a, b).astype(F32)
        out[rows + n : rows + 2 * n, cols : cols + 256] = jnp.where(own, b, a).astype(F32)

    for k in range(BANDS):
        place(band.at[k], 0, 256, k * 512, 0)
        place(band.at[k], 0, 256, k * 512 + 256, 256)
    place(point, 0, 256, 2048, 0)
    place(point, 0, 256, 2304, 256)
    place(proj, 0, 256, 2560, 0)
    for t in range(TAPS):
        place(conv.at[t], 0, 128, EARLY + t * 128, 0)


def finish_pass(core, mine, other):
    vm = pl.BlockSpec(memory_space=pltpu.VMEM)
    return pl.pallas_call(
        finish_kernel,
        in_specs=[pl.BlockSpec(memory_space=pltpu.SMEM), vm, vm],
        out_specs=[vm] * 4,
        out_shape=[
            jax.ShapeDtypeStruct((TAPS, CF, CF), F32),
            jax.ShapeDtypeStruct((BANDS, C, C), F32),
            jax.ShapeDtypeStruct((C, C), F32),
            jax.ShapeDtypeStruct((C, CF), F32),
        ],
        compiler_params=pltpu.CompilerParams(vmem_limit_bytes=VMEM),
        name="place_gradients",
    )(core, mine, other)


def neighbours(axes, count):
    forward = [(i, i + 1) for i in range(count - 1)]
    return forward, [(b, a) for a, b in forward]


def halo(tile):
    forward, backward = neighbours(COL, 16)
    west = lax.ppermute(tile[:, TC - 1 :], COL, forward)
    east = lax.ppermute(tile[:, :1], COL, backward)
    forward, backward = neighbours(ROW, 8)
    low = jnp.concatenate([tile[TR - 1 :], west[TR - 1 :], east[TR - 1 :]], axis=1)
    high = jnp.concatenate([tile[:1], west[:1], east[:1]], axis=1)
    above = lax.ppermute(low, ROW, forward)
    below = lax.ppermute(high, ROW, backward)
    left = jnp.concatenate([above[:, TC : TC + 1], west, below[:, TC : TC + 1]], axis=0)
    right = jnp.concatenate([above[:, TC + 1 :], east, below[:, TC + 1 :]], axis=0)
    return above[:, :TC].astype(F32), below[:, :TC].astype(F32), left.astype(F32), right.astype(F32)


def local(coarse_in, fine_in, band_weight, point_weight, proj_weight, conv_weight, out_cot):
    core = lax.axis_index("c").astype(jnp.int32).reshape(1)
    haar = jnp.asarray(haar_matrix(), BF)
    x = lax.all_to_all(coarse_in, COL, 1, 0, tiled=True).reshape(CELLS, C)
    top, bot, left, right = halo(out_cot)
    shifted, dco = cot_pass(out_cot, top, bot, left, right, conv_weight)
    sub, pre, hidden, cout = coarse_pass(x, haar, band_weight, point_weight, proj_weight)
    conv_in, keep_late, send_late = wgrad_pass(core, fine_in, cout, shifted)
    keep_early, send_early = grads_pass(core, x, haar, proj_weight, sub, pre, hidden, dco)
    swap = [(0, 1), (1, 0)]
    got_late = lax.ppermute(send_late, "c", swap)
    got_early = lax.ppermute(send_early, "c", swap)
    chip = jnp.concatenate(
        [
            keep_early.astype(F32) + got_early.astype(F32),
            keep_late.astype(F32) + got_late.astype(F32),
            jnp.zeros((PACK - EARLY - LATE, 256), F32),
        ]
    ).astype(BF)
    parts = lax.all_to_all(chip, CHIPS, 0, 0, tiled=True).reshape(PEERS, PACK // PEERS, 256)
    done = (jnp.sum(parts.astype(F32), axis=0) * SCALE).astype(BF)
    spread = jnp.broadcast_to(done[None], (PEERS, PACK // PEERS, 256)).reshape(PACK, 256)
    mine = lax.all_to_all(spread, CHIPS, 0, 0, tiled=True)
    other = lax.ppermute(mine, "c", swap)
    grad_conv, grad_band, grad_point, grad_proj = finish_pass(core, mine, other)
    fine_out = conv_pass(conv_in, *halo(conv_in), conv_weight)
    return fine_out, grad_conv, grad_band, grad_point, grad_proj


def solution(mesh):
    fine_mesh = Mesh(
        np.asarray(mesh.devices).reshape([n for _, n in GRID]), tuple(name for name, _ in GRID)
    )
    fine = P(ROW, COL, None)
    in_specs = (P(ROW + COL, None, None), fine, P(), P(), P(), P(), fine)
    out_specs = (fine, P(), P(), P(), P())
    return jax.shard_map(local, mesh=fine_mesh, in_specs=in_specs, out_specs=out_specs, check_vma=False)
```

```python
import functools

import jax
import jax.numpy as jnp
import numpy as np
from jax import lax
from jax.experimental import pallas as pl
from jax.experimental.pallas import tpu as pltpu
from jax.sharding import Mesh
from jax.sharding import PartitionSpec as P

BF = jnp.bfloat16
F32 = jnp.float32
ROW = ("xl", "z")
COL = ("xh", "y", "c")
CHIPS = ("xl", "z", "xh", "y")
GRID = (("xl", 2), ("z", 4), ("xh", 2), ("y", 4), ("c", 2))

C, CF, BANDS, TAPS = 512, 256, 4, 9
TR, TC = 128, 32
IR, IC = 32, 8
CELLS = IR * IC
PAIR = 2 * CELLS
HB = 32
NB = TR // HB
SIDE = 136
EARLY = 5 * 4 * 256 + 2 * 256
LATE = TAPS * 2 * 128
PEERS = 64
SCALE = float(1024 * 512) ** (-0.5)
MIB = 1024 * 1024
GELU_A = 0.7978845608028654
GELU_B = 0.044715


def params(mib, grid=1):
    return pltpu.CompilerParams(
        vmem_limit_bytes=mib * MIB, dimension_semantics=("arbitrary",) * grid if grid else None
    )


def cost(flops, moved):
    return pl.CostEstimate(flops=flops, bytes_accessed=moved, transcendentals=0)


def whole(*shape):
    return pl.BlockSpec(shape, lambda i: (0,) * len(shape))


def dot(a, b, dims=((1,), (0,))):
    return lax.dot_general(a, b, (dims, ((), ())), preferred_element_type=F32)


def haar_matrix():
    out = np.zeros((BANDS, 8, 8, 16, 16), np.float32)
    signs = ((1, 1, 1, 1), (1, -1, 1, -1), (1, 1, -1, -1), (1, -1, -1, 1))
    for k in range(BANDS):
        for i in range(8):
            for j in range(8):
                for t in range(4):
                    out[k, i, j, 2 * i + t // 2, 2 * j + t % 2] = 0.5 * signs[k][t]
    return out.reshape(256, 256)


def pool_matrices():
    inner = np.zeros((3, 3, IC, 6, TC), np.float32)
    side = np.zeros((3, IR, SIDE), np.float32)
    for a in range(3):
        for b in range(3):
            for j in range(IC):
                low, high = max(4 * j - b + 1, 0), min(4 * j - b + 4, TC - 1)
                inner[a, b, j, 2 - a : 6 - a, low : high + 1] = 1
        for i in range(IR):
            side[a, i, 4 * i + 2 - a : 4 * i + 6 - a] = 1
    return inner.reshape(TAPS * IC, 6 * TC), side.reshape(3 * IR, SIDE)


def dcoarse_kernel(oc, rows, left, right, inner, side, wconv, out, pooled):
    pool = inner[...]
    for i in range(IR):
        if i == 0:
            block = jnp.concatenate([rows[0], oc[: 5 * TC, :]], axis=0)
        elif i == IR - 1:
            block = jnp.concatenate([oc[(4 * i - 1) * TC :, :], rows[1]], axis=0)
        else:
            block = oc[(4 * i - 1) * TC : (4 * i + 5) * TC, :]
        part = dot(pool, block)
        for t in range(TAPS):
            for h in range(2):
                pooled[t, h, i * IC : (i + 1) * IC, :] = part[t * IC : (t + 1) * IC, h * 128 : (h + 1) * 128]
    for edge, b, start in ((left, 2, 0), (right, 0, IC - 1)):
        part = dot(side[...], edge[...].astype(BF))
        for a in range(3):
            for h in range(2):
                cells = pl.ds(start, IR, stride=IC)
                pooled[3 * a + b, h, cells, :] += part[a * IR : (a + 1) * IR, h * 128 : (h + 1) * 128]
    total = jnp.zeros((CELLS, CF), F32)
    for t in range(TAPS):
        s = jnp.concatenate([pooled[t, 0], pooled[t, 1]], axis=-1).astype(BF)
        total += dot(s, wconv[t], ((1,), (1,)))
    out[...] = total.astype(BF)


def dcoarse_pass(oc, rows, left, right, wconv):
    inner, side = pool_matrices()
    vm = pl.BlockSpec(memory_space=pltpu.VMEM)
    return pl.pallas_call(
        dcoarse_kernel,
        in_specs=[vm] * 7,
        out_specs=vm,
        out_shape=jax.ShapeDtypeStruct((CELLS, CF), BF),
        scratch_shapes=[pltpu.VMEM((TAPS, 2, CELLS, 128), F32)],
        compiler_params=params(20, 0),
        cost_estimate=cost(600_000_000, 4_000_000),
        name="coarse_cotangent",
    )(oc.reshape(TR * TC, CF), rows, left, right, jnp.asarray(inner, BF), jnp.asarray(side, BF), wconv)


def coarse_kernel(core, x, haar, wband, wpoint, wproj, sub, pre, hidden, cout, split, outs):
    k = pl.program_id(0)
    h = haar[pl.ds(pl.multiple_of(k * 64, 64), 64), :]
    part = jnp.concatenate([dot(h, x[:256, :]), dot(h, x[256:, :])], axis=0).astype(BF)
    sub[pl.ds(pl.multiple_of(k * 128, 128), 128), :] = part
    m = dot(part, wband[0])
    hi = m.astype(BF)
    lo = (m - hi.astype(F32)).astype(BF)
    rows = pl.ds(pl.multiple_of(k * 64, 64), 64)
    for g in range(2):
        split[g, 0, rows, :] = hi[g * 64 : (g + 1) * 64]
        split[g, 1, rows, :] = lo[g * 64 : (g + 1) * 64]

    @pl.when(k == BANDS - 1)
    def _():
        h = haar[...]
        for g in range(2):
            cells = slice(g * 256, (g + 1) * 256)
            value = dot(h, split[g, 0], ((0,), (0,))) + dot(h, split[g, 1], ((0,), (0,)))
            value = value + dot(x[cells, :], wpoint[...])
            pre[cells, :] = value
            act = 0.5 * value * (1.0 + jnp.tanh(GELU_A * (value + GELU_B * (value * value * value))))
            act = act.astype(BF)
            hidden[cells, :] = act
            outs[g * 16 : (g + 1) * 16] = dot(act, wproj[...]).reshape(16, 16, CF)
        own = outs[:, pl.ds(pl.multiple_of(core[0] * IC, IC), IC), :]
        cout[...] = own.reshape(CELLS, CF).astype(BF)


def coarse_pass(core, x, haar, wband, wpoint, wproj):
    return pl.pallas_call(
        coarse_kernel,
        grid=(BANDS,),
        in_specs=[
            pl.BlockSpec(memory_space=pltpu.SMEM),
            whole(PAIR, C),
            whole(256, 256),
            pl.BlockSpec((1, C, C), lambda i: (i, 0, 0)),
            whole(C, C),
            whole(C, CF),
        ],
        out_specs=[whole(PAIR, C), whole(PAIR, C), whole(PAIR, C), whole(CELLS, CF)],
        out_shape=[
            jax.ShapeDtypeStruct((PAIR, C), BF),
            jax.ShapeDtypeStruct((PAIR, C), F32),
            jax.ShapeDtypeStruct((PAIR, C), BF),
            jax.ShapeDtypeStruct((CELLS, CF), BF),
        ],
        scratch_shapes=[pltpu.VMEM((2, 2, 256, C), BF), pltpu.VMEM((IR, 2 * IC, CF), F32)],
        compiler_params=params(24),
        cost_estimate=cost(1_000_000_000, 6_000_000),
        name="coarse_forward",
    )(core, x, haar, wband, wpoint, wproj)


def grads_kernel(core, x, haar, wproj, sub, pre, hidden, dco, dtwin, out, both):
    own = pl.multiple_of(core[0] * IC, IC)
    both[:, pl.ds(own, IC), :] = dco[...].astype(F32).reshape(IR, IC, CF)
    both[:, pl.ds(IC - own, IC), :] = dtwin[...].astype(F32).reshape(IR, IC, CF)
    d = both[...].reshape(PAIR, CF).astype(BF)
    value = pre[...]
    square = value * value
    th = jnp.tanh(GELU_A * (value + GELU_B * (value * square)))
    slope = 0.5 * (1.0 + th) + 0.5 * value * (1.0 - th * th) * (GELU_A * (1.0 + 3.0 * GELU_B * square))
    dpre = (dot(d, wproj[...], ((1,), (1,))) * slope).astype(BF)
    h = haar[...]
    dmix = [dot(h, dpre[g * 256 : (g + 1) * 256]).astype(BF) for g in range(2)]
    half = pl.ds(pl.multiple_of(core[0] * 256, 256), 256)
    for k in range(5):
        if k < BANDS:
            dk = jnp.concatenate([dmix[g][k * 64 : (k + 1) * 64] for g in range(2)], axis=0)
            grad = dot(sub[k * 128 : (k + 1) * 128, half], dk, ((0,), (0,)))
        else:
            grad = dot(x[:, half], dpre, ((0,), (0,)))
        for n in range(4):
            at = (4 * k + n) * 256
            out[at : at + 256, :] = grad[:, n * 128 : (n + 1) * 128].astype(BF)
    grad = dot(hidden[:, half], d, ((0,), (0,)))
    for n in range(2):
        at = (20 + n) * 256
        out[at : at + 256, :] = grad[:, n * 128 : (n + 1) * 128].astype(BF)


def grads_pass(core, x, haar, wproj, sub, pre, hidden, dco, dtwin):
    vm = pl.BlockSpec(memory_space=pltpu.VMEM)
    return pl.pallas_call(
        grads_kernel,
        in_specs=[pl.BlockSpec(memory_space=pltpu.SMEM)] + [vm] * 8,
        out_specs=vm,
        out_shape=jax.ShapeDtypeStruct((EARLY, 128), BF),
        scratch_shapes=[pltpu.VMEM((IR, 2 * IC, CF), F32)],
        compiler_params=params(24, 0),
        cost_estimate=cost(1_000_000_000, 6_000_000),
        name="coarse_gradients",
    )(core, x, haar, wproj, sub, pre, hidden, dco, dtwin)


def fill_windows(i, tile, rows, left, right, win):
    r0 = i * HB
    win[1 : HB + 1, 8 : 8 + TC, :] = tile[pl.ds(r0, HB)].astype(F32)
    before = tile[pl.ds(jnp.maximum(r0 - 1, 0), 1)].astype(F32)
    after = tile[pl.ds(jnp.minimum(r0 + HB, TR - 1), 1)].astype(F32)
    win[0:1, 8 : 8 + TC, :] = jnp.where(i == 0, rows[0:1].astype(F32), before)
    win[HB + 1 : HB + 2, 8 : 8 + TC, :] = jnp.where(i == NB - 1, rows[1:2].astype(F32), after)
    for r in range(HB + 2):
        win[r, 7:8, :] = left[pl.ds(r0 + r, 1), :]
        win[r, 8 + TC : 9 + TC, :] = right[pl.ds(r0 + r, 1), :]


def wgrad_kernel(core, fine, cout, oc, rows, left, right, conv_in, keep, send, up, win, shifted, acc):
    i = pl.program_id(0)
    for q in range(HB // 4):
        cell = cout[q * IC : (q + 1) * IC, :].astype(F32)
        for s in range(4):
            up[q, 0, pl.ds(s, IC, stride=4), :] = cell[:, :128]
            up[q, 1, pl.ds(s, IC, stride=4), :] = cell[:, 128:]
        grown = jnp.concatenate([up[q, 0], up[q, 1]], axis=-1)
        for t in range(4):
            conv_in[4 * q + t] = (fine[4 * q + t].astype(F32) + grown).astype(BF)
    fill_windows(i, oc, rows, left, right, win)
    for b in range(3):
        shifted[:, :, b * CF : (b + 1) * CF] = win[:, 9 - b : 9 - b + TC, :].astype(BF)

    @pl.when(i == 0)
    def _():
        acc[...] = jnp.zeros_like(acc)

    cells = conv_in[...].reshape(HB * TC, CF).T
    for a in range(3):
        acc[a] += dot(cells, shifted[2 - a : 2 - a + HB].reshape(HB * TC, 3 * CF))

    @pl.when(i == NB - 1)
    def _():
        for out, c in ((keep, core[0]), (send, 1 - core[0])):
            half = pl.ds(pl.multiple_of(c * 128, 128), 128)
            for t in range(TAPS):
                for n in range(2):
                    at = (t % 3) * CF + n * 128
                    out[(2 * t + n) * 128 : (2 * t + n + 1) * 128, :] = acc[t // 3, half, at : at + 128].astype(BF)


def wgrad_pass(core, fine, cout, oc, rows, left, right):
    return pl.pallas_call(
        wgrad_kernel,
        grid=(NB,),
        in_specs=[
            pl.BlockSpec(memory_space=pltpu.SMEM),
            pl.BlockSpec((HB, TC, CF), lambda i: (i, 0, 0)),
            pl.BlockSpec((HB // 4 * IC, CF), lambda i: (i, 0)),
            whole(TR, TC, CF),
            whole(2, TC, CF),
            whole(SIDE, CF),
            whole(SIDE, CF),
        ],
        out_specs=[
            pl.BlockSpec((HB, TC, CF), lambda i: (i, 0, 0)),
            whole(LATE, 128),
            whole(LATE, 128),
        ],
        out_shape=[
            jax.ShapeDtypeStruct((TR, TC, CF), BF),
            jax.ShapeDtypeStruct((LATE, 128), BF),
            jax.ShapeDtypeStruct((LATE, 128), BF),
        ],
        scratch_shapes=[
            pltpu.VMEM((HB // 4, 2, TC, 128), F32),
            pltpu.VMEM((HB + 2, 48, CF), F32),
            pltpu.VMEM((HB + 2, TC, 3 * CF), BF),
            pltpu.VMEM((3, CF, 3 * CF), F32),
        ],
        compiler_params=params(32),
        cost_estimate=cost(8_000_000_000, 9_000_000),
        name="conv_weight_gradient",
    )(core, fine, cout, oc, rows, left, right)


def conv_kernel(ci, rows, left, right, wconv, out, win, wide):
    i = pl.program_id(0)
    fill_windows(i, ci, rows, left, right, win)
    for b in range(3):
        wide[:, :, b * CF : (b + 1) * CF] = win[:, 7 + b : 7 + b + TC, :].astype(BF)
    total = jnp.zeros((HB * TC, CF), F32)
    for a in range(3):
        total += dot(wide[a : a + HB].reshape(HB * TC, 3 * CF), wconv[a])
    out[...] = total.astype(BF).reshape(HB, TC, CF)


def conv_pass(ci, rows, left, right, wconv):
    return pl.pallas_call(
        conv_kernel,
        grid=(NB,),
        in_specs=[
            whole(TR, TC, CF),
            whole(2, TC, CF),
            whole(SIDE, CF),
            whole(SIDE, CF),
            whole(3, 3 * CF, CF),
        ],
        out_specs=pl.BlockSpec((HB, TC, CF), lambda i: (i, 0, 0)),
        out_shape=jax.ShapeDtypeStruct((TR, TC, CF), BF),
        scratch_shapes=[pltpu.VMEM((HB + 2, 48, CF), F32), pltpu.VMEM((HB + 2, TC, 3 * CF), BF)],
        compiler_params=params(32),
        cost_estimate=cost(8_000_000_000, 6_000_000),
        name="conv_forward",
    )(ci, rows, left, right, wconv.reshape(3, 3 * CF, CF))


def small_call(kernel, name, outs, *args):
    vm = pl.BlockSpec(memory_space=pltpu.VMEM)
    return pl.pallas_call(
        kernel,
        in_specs=[pl.BlockSpec(memory_space=pltpu.SMEM)] + [vm] * (len(args) - 1),
        out_specs=[vm] * len(outs),
        out_shape=[jax.ShapeDtypeStruct(s, BF) for s in outs],
        compiler_params=params(16, 0),
        name=name,
    )(*args)


def deal_kernel(at, *refs):
    ins, outs = refs[:-4], refs[-4:]
    n = outs[0].shape[0]
    for d in range(4):
        rows = pl.ds(pl.multiple_of(lax.rem(at[0] + d, 4) * n, n), n)
        total = ins[0][rows, :].astype(F32)
        for r in ins[1:]:
            total = total + r[rows, :].astype(F32)
        outs[d][...] = total.astype(BF)


def deal(at, *ins):
    n = ins[0].shape[0] // 4
    return small_call(deal_kernel, "sum_and_deal", [(n, 128)] * 4, at, *ins)


def add_kernel(at, *refs):
    total = refs[0][...].astype(F32)
    for r in refs[1:-1]:
        total = total + r[...].astype(F32)
    refs[-1][...] = total.astype(BF)


def add(at, *ins):
    return small_call(add_kernel, "sum_parts", [ins[0].shape], at, *ins)[0]


def ordered_sum_kernel(at, own, r1, r2, r3, out, slots):
    for d, r in enumerate((own, r1, r2, r3)):
        slots[lax.rem(at[0] + 4 - d, 4)] = r[...].astype(F32)
    out[...] = (((slots[0] + slots[1]) + (slots[2] + slots[3])) * SCALE).astype(BF)


def ordered_sum(at, *ins):
    vm = pl.BlockSpec(memory_space=pltpu.VMEM)
    shape = ins[0].shape
    return pl.pallas_call(
        ordered_sum_kernel,
        in_specs=[pl.BlockSpec(memory_space=pltpu.SMEM)] + [vm] * 4,
        out_specs=vm,
        out_shape=jax.ShapeDtypeStruct(shape, BF),
        scratch_shapes=[pltpu.VMEM((4,) + shape, F32)],
        compiler_params=params(16, 0),
        name="ordered_sum",
    )(at, *ins)


def gather_kernel(at, own, r1, r2, r3, out):
    n = own.shape[0]
    for d, r in enumerate((own, r1, r2, r3)):
        rows = pl.ds(pl.multiple_of(lax.rem(at[0] + 4 - d, 4) * n, n), n)
        out[rows, :] = r[...]


def gather(at, *ins):
    n = ins[0].shape[0]
    return small_call(gather_kernel, "place_parts", [(4 * n, 128)], at, *ins)[0]


def ring(parts, axes):
    return [lax.ppermute(p, axes, [(i, (i + d + 1) % 4) for i in range(4)]) for d, p in enumerate(parts)]


def finish_kernel(core, mine, other, mine_late, other_late, conv, band, point, proj):
    own = core[0] == 0

    def place(out, n, a, b, start, cols):
        a, b = a[start : start + n, :], b[start : start + n, :]
        out[0:n, cols : cols + 128] = jnp.where(own, a, b).astype(F32)
        out[n : 2 * n, cols : cols + 128] = jnp.where(own, b, a).astype(F32)

    for k in range(5):
        for n in range(4):
            place(band.at[k] if k < BANDS else point, 256, mine, other, (4 * k + n) * 256, 128 * n)
    for n in range(2):
        place(proj, 256, mine, other, (20 + n) * 256, 128 * n)
    for t in range(TAPS):
        for n in range(2):
            place(conv.at[t], 128, mine_late, other_late, (2 * t + n) * 128, 128 * n)


def finish_pass(core, *ins):
    vm = pl.BlockSpec(memory_space=pltpu.VMEM)
    return pl.pallas_call(
        finish_kernel,
        in_specs=[pl.BlockSpec(memory_space=pltpu.SMEM)] + [vm] * 4,
        out_specs=[vm] * 4,
        out_shape=[
            jax.ShapeDtypeStruct((TAPS, CF, CF), F32),
            jax.ShapeDtypeStruct((BANDS, C, C), F32),
            jax.ShapeDtypeStruct((C, C), F32),
            jax.ShapeDtypeStruct((C, CF), F32),
        ],
        compiler_params=params(24, 0),
        name="place_gradients",
    )(core, *ins)


def neighbours(axes, count):
    forward = [(i, i + 1) for i in range(count - 1)]
    return forward, [(b, a) for a, b in forward]


def halo(tile, east_edge, west_edge):
    forward, backward = neighbours(COL, 16)
    west = lax.ppermute(east_edge, COL, forward)
    east = lax.ppermute(west_edge, COL, backward)
    forward, backward = neighbours(ROW, 8)
    low = jnp.concatenate([tile[TR - 1], west[TR - 1 :], east[TR - 1 :]], axis=0)
    high = jnp.concatenate([tile[0], west[:1], east[:1]], axis=0)
    above = lax.ppermute(low, ROW, forward)
    below = lax.ppermute(high, ROW, backward)
    pad = jnp.zeros((SIDE - TR - 2, CF), BF)
    left = jnp.concatenate([above[TC : TC + 1], west, below[TC : TC + 1], pad], axis=0)
    right = jnp.concatenate([above[TC + 1 :], east, below[TC + 1 :], pad], axis=0)
    return jnp.stack([above[:TC], below[:TC]]), left.astype(F32), right.astype(F32)


def local(coarse_in, fine_in, band_weight, point_weight, proj_weight, conv_weight, out_cot):
    index = lambda axes: lax.axis_index(axes).astype(jnp.int32).reshape(1)
    core, at_y, at_z, at_x = index("c"), index("y"), index("z"), index(("xl", "xh"))
    swap = [(0, 1), (1, 0)]
    haar = jnp.asarray(haar_matrix(), BF)

    chunks = coarse_in.reshape(2, 8, 16, C).transpose(1, 0, 2, 3)
    chunks = jnp.broadcast_to(chunks[:, None], (8, 2, 2, 16, C)).reshape(16, 2, 16, C)
    x = lax.all_to_all(chunks, COL, 0, 0, tiled=True).reshape(PAIR, C)
    cot_halo = halo(out_cot, out_cot[:, TC - 1], out_cot[:, 0])
    sub, pre, hidden, cout = coarse_pass(core, x, haar, band_weight, point_weight, proj_weight)
    dco = dcoarse_pass(out_cot, *cot_halo, conv_weight)
    dtwin = lax.ppermute(dco, "c", swap)
    early = grads_pass(core, x, haar, proj_weight, sub, pre, hidden, dco, dtwin)

    parts = lax.all_to_all(early, CHIPS, 0, 0, tiled=True)
    conv_in, keep, send = wgrad_pass(core, fine_in, cout, out_cot, *cot_halo)
    got = lax.ppermute(send, "c", swap)
    own, *away = deal(at_y, keep, got)
    own, *away = deal(at_z, own, *ring(away, "y"))
    own = add(at_z, own, *ring(away, "z"))
    own = ordered_sum(at_x, own, *ring([own] * 3, ("xl", "xh")))

    parts = parts.reshape(PEERS, EARLY // PEERS, 128)
    done = (jnp.sum(parts.astype(F32), axis=0) * SCALE).astype(BF)
    spread = jnp.broadcast_to(done[None], (PEERS, EARLY // PEERS, 128)).reshape(EARLY, 128)
    mine = lax.all_to_all(spread, CHIPS, 0, 0, tiled=True)

    own = gather(at_z, own, *ring([own] * 3, "z"))
    mine_late = gather(at_y, own, *ring([own] * 3, "y"))
    other_late = lax.ppermute(mine_late, "c", swap)
    other = lax.ppermute(mine, "c", swap)
    fine_out = conv_pass(conv_in, *halo(conv_in, conv_in[:, TC - 1], conv_in[:, 0]), conv_weight)
    grad_conv, grad_band, grad_point, grad_proj = finish_pass(core, mine, other, mine_late, other_late)
    return fine_out, grad_conv, grad_band, grad_point, grad_proj


def solution(mesh):
    fine_mesh = Mesh(
        np.asarray(mesh.devices).reshape([n for _, n in GRID]), tuple(name for name, _ in GRID)
    )
    fine = P(ROW, COL, None)
    in_specs = (P(ROW + COL, None, None), fine, P(), P(), P(), P(), fine)
    out_specs = (fine, P(), P(), P(), P())
    return jax.shard_map(local, mesh=fine_mesh, in_specs=in_specs, out_specs=out_specs, check_vma=False)
```

```python
import functools

import jax
import jax.numpy as jnp
import numpy as np
from jax import lax
from jax.experimental import pallas as pl
from jax.experimental.pallas import tpu as pltpu
from jax.sharding import Mesh
from jax.sharding import PartitionSpec as P

BF = jnp.bfloat16
F32 = jnp.float32
ROW = ("xl", "z")
COL = ("xh", "y", "c")
CHIPS = ("xl", "z", "xh", "y")
GRID = (("xl", 2), ("z", 4), ("xh", 2), ("y", 4), ("c", 2))

C, CF, BANDS, TAPS = 512, 256, 4, 9
TR, TC = 128, 32
IR, IC = 32, 8
CELLS = IR * IC
PAIR = 2 * CELLS
HB = 32
NB = TR // HB
SIDE = 136
LATE = TAPS * 2 * 128 + 256
EARLY = 5 * 4 * 256 + 2 * 256
PACK = LATE + EARLY
PEERS = 64
SCALE = float(1024 * 512) ** (-0.5)
MIB = 1024 * 1024
GELU_A = 0.7978845608028654
GELU_B = 0.044715


def params(mib, grid=1):
    return pltpu.CompilerParams(
        vmem_limit_bytes=mib * MIB, dimension_semantics=("arbitrary",) * grid if grid else None
    )


def cost(flops, moved):
    return pl.CostEstimate(flops=flops, bytes_accessed=moved, transcendentals=0)


def whole(*shape):
    return pl.BlockSpec(shape, lambda i: (0,) * len(shape))


def dot(a, b, dims=((1,), (0,))):
    return lax.dot_general(a, b, (dims, ((), ())), preferred_element_type=F32)


def haar_matrix():
    out = np.zeros((BANDS, 8, 8, 16, 16), np.float32)
    signs = ((1, 1, 1, 1), (1, -1, 1, -1), (1, 1, -1, -1), (1, -1, -1, 1))
    for k in range(BANDS):
        for i in range(8):
            for j in range(8):
                for t in range(4):
                    out[k, i, j, 2 * i + t // 2, 2 * j + t % 2] = 0.5 * signs[k][t]
    return out.reshape(256, 256)


def pool_matrices():
    inner = np.zeros((3, 3, IC, 6, TC), np.float32)
    side = np.zeros((3, IR, SIDE), np.float32)
    for a in range(3):
        for b in range(3):
            for j in range(IC):
                low, high = max(4 * j - b + 1, 0), min(4 * j - b + 4, TC - 1)
                inner[a, b, j, 2 - a : 6 - a, low : high + 1] = 1
        for i in range(IR):
            side[a, i, 4 * i + 2 - a : 4 * i + 6 - a] = 1
    return inner.reshape(TAPS * IC, 6 * TC), side.reshape(3 * IR, SIDE)


def dcoarse_kernel(oc, rows, left, right, inner, side, wconv, out, pooled):
    pool = inner[...]
    for i in range(IR):
        if i == 0:
            block = jnp.concatenate([rows[0], oc[: 5 * TC, :]], axis=0)
        elif i == IR - 1:
            block = jnp.concatenate([oc[(4 * i - 1) * TC :, :], rows[1]], axis=0)
        else:
            block = oc[(4 * i - 1) * TC : (4 * i + 5) * TC, :]
        part = dot(pool, block)
        for t in range(TAPS):
            for h in range(2):
                pooled[t, h, i * IC : (i + 1) * IC, :] = part[t * IC : (t + 1) * IC, h * 128 : (h + 1) * 128]
    for edge, b, start in ((left, 2, 0), (right, 0, IC - 1)):
        part = dot(side[...], edge[...].astype(BF))
        for a in range(3):
            for h in range(2):
                cells = pl.ds(start, IR, stride=IC)
                pooled[3 * a + b, h, cells, :] += part[a * IR : (a + 1) * IR, h * 128 : (h + 1) * 128]
    total = jnp.zeros((CELLS, CF), F32)
    for t in range(TAPS):
        s = jnp.concatenate([pooled[t, 0], pooled[t, 1]], axis=-1).astype(BF)
        total += dot(s, wconv[t], ((1,), (1,)))
    out[...] = total.astype(BF)


def dcoarse_pass(oc, rows, left, right, wconv):
    inner, side = pool_matrices()
    vm = pl.BlockSpec(memory_space=pltpu.VMEM)
    return pl.pallas_call(
        dcoarse_kernel,
        in_specs=[vm] * 7,
        out_specs=vm,
        out_shape=jax.ShapeDtypeStruct((CELLS, CF), BF),
        scratch_shapes=[pltpu.VMEM((TAPS, 2, CELLS, 128), F32)],
        compiler_params=params(20, 0),
        cost_estimate=cost(600_000_000, 4_000_000),
        name="coarse_cotangent",
    )(oc.reshape(TR * TC, CF), rows, left, right, jnp.asarray(inner, BF), jnp.asarray(side, BF), wconv)


def coarse_kernel(core, x, haar, wband, wpoint, wproj, sub, pre, hidden, cout, split, outs):
    k = pl.program_id(0)
    h = haar[pl.ds(pl.multiple_of(k * 64, 64), 64), :]
    part = jnp.concatenate([dot(h, x[:256, :]), dot(h, x[256:, :])], axis=0).astype(BF)
    sub[pl.ds(pl.multiple_of(k * 128, 128), 128), :] = part
    m = dot(part, wband[0])
    hi = m.astype(BF)
    lo = (m - hi.astype(F32)).astype(BF)
    rows = pl.ds(pl.multiple_of(k * 64, 64), 64)
    for g in range(2):
        split[g, 0, rows, :] = hi[g * 64 : (g + 1) * 64]
        split[g, 1, rows, :] = lo[g * 64 : (g + 1) * 64]

    @pl.when(k == BANDS - 1)
    def _():
        h = haar[...]
        for g in range(2):
            cells = slice(g * 256, (g + 1) * 256)
            value = dot(h, split[g, 0], ((0,), (0,))) + dot(h, split[g, 1], ((0,), (0,)))
            value = value + dot(x[cells, :], wpoint[...])
            pre[cells, :] = value
            act = 0.5 * value * (1.0 + jnp.tanh(GELU_A * (value + GELU_B * (value * value * value))))
            act = act.astype(BF)
            hidden[cells, :] = act
            outs[g * 16 : (g + 1) * 16] = dot(act, wproj[...]).reshape(16, 16, CF)
        own = outs[:, pl.ds(pl.multiple_of(core[0] * IC, IC), IC), :]
        cout[...] = own.reshape(CELLS, CF).astype(BF)


def coarse_pass(core, x, haar, wband, wpoint, wproj):
    return pl.pallas_call(
        coarse_kernel,
        grid=(BANDS,),
        in_specs=[
            pl.BlockSpec(memory_space=pltpu.SMEM),
            whole(PAIR, C),
            whole(256, 256),
            pl.BlockSpec((1, C, C), lambda i: (i, 0, 0)),
            whole(C, C),
            whole(C, CF),
        ],
        out_specs=[whole(PAIR, C), whole(PAIR, C), whole(PAIR, C), whole(CELLS, CF)],
        out_shape=[
            jax.ShapeDtypeStruct((PAIR, C), BF),
            jax.ShapeDtypeStruct((PAIR, C), F32),
            jax.ShapeDtypeStruct((PAIR, C), BF),
            jax.ShapeDtypeStruct((CELLS, CF), BF),
        ],
        scratch_shapes=[pltpu.VMEM((2, 2, 256, C), BF), pltpu.VMEM((IR, 2 * IC, CF), F32)],
        compiler_params=params(24),
        cost_estimate=cost(1_000_000_000, 6_000_000),
        name="coarse_forward",
    )(core, x, haar, wband, wpoint, wproj)


def grads_kernel(core, x, haar, wproj, sub, pre, hidden, dco, dtwin, out, both):
    own = pl.multiple_of(core[0] * IC, IC)
    both[:, pl.ds(own, IC), :] = dco[...].astype(F32).reshape(IR, IC, CF)
    both[:, pl.ds(IC - own, IC), :] = dtwin[...].astype(F32).reshape(IR, IC, CF)
    d = both[...].reshape(PAIR, CF).astype(BF)
    value = pre[...]
    square = value * value
    th = jnp.tanh(GELU_A * (value + GELU_B * (value * square)))
    slope = 0.5 * (1.0 + th) + 0.5 * value * (1.0 - th * th) * (GELU_A * (1.0 + 3.0 * GELU_B * square))
    dpre = (dot(d, wproj[...], ((1,), (1,))) * slope).astype(BF)
    h = haar[...]
    dmix = [dot(h, dpre[g * 256 : (g + 1) * 256]).astype(BF) for g in range(2)]
    half = pl.ds(pl.multiple_of(core[0] * 256, 256), 256)
    for k in range(5):
        if k < BANDS:
            dk = jnp.concatenate([dmix[g][k * 64 : (k + 1) * 64] for g in range(2)], axis=0)
            grad = dot(sub[k * 128 : (k + 1) * 128, half], dk, ((0,), (0,)))
        else:
            grad = dot(x[:, half], dpre, ((0,), (0,)))
        for n in range(4):
            at = LATE + (4 * k + n) * 256
            out[at : at + 256, :] = grad[:, n * 128 : (n + 1) * 128].astype(BF)
    grad = dot(hidden[:, half], d, ((0,), (0,)))
    for n in range(2):
        at = LATE + (20 + n) * 256
        out[at : at + 256, :] = grad[:, n * 128 : (n + 1) * 128].astype(BF)


def grads_pass(core, x, haar, wproj, sub, pre, hidden, dco, dtwin):
    vm = pl.BlockSpec(memory_space=pltpu.VMEM)
    return pl.pallas_call(
        grads_kernel,
        in_specs=[pl.BlockSpec(memory_space=pltpu.SMEM)] + [vm] * 8,
        out_specs=vm,
        out_shape=jax.ShapeDtypeStruct((PACK, 128), BF),
        scratch_shapes=[pltpu.VMEM((IR, 2 * IC, CF), F32)],
        compiler_params=params(24, 0),
        cost_estimate=cost(1_000_000_000, 6_000_000),
        name="coarse_gradients",
    )(core, x, haar, wproj, sub, pre, hidden, dco, dtwin)


def fill_windows(i, tile, rows, left, right, win):
    r0 = i * HB
    win[1 : HB + 1, 8 : 8 + TC, :] = tile[pl.ds(r0, HB)].astype(F32)
    before = tile[pl.ds(jnp.maximum(r0 - 1, 0), 1)].astype(F32)
    after = tile[pl.ds(jnp.minimum(r0 + HB, TR - 1), 1)].astype(F32)
    win[0:1, 8 : 8 + TC, :] = jnp.where(i == 0, rows[0:1].astype(F32), before)
    win[HB + 1 : HB + 2, 8 : 8 + TC, :] = jnp.where(i == NB - 1, rows[1:2].astype(F32), after)
    for r in range(HB + 2):
        win[r, 7:8, :] = left[pl.ds(r0 + r, 1), :]
        win[r, 8 + TC : 9 + TC, :] = right[pl.ds(r0 + r, 1), :]


def wgrad_kernel(core, fine, cout, oc, rows, left, right, conv_in, keep, send, up, win, shifted, acc):
    i = pl.program_id(0)
    coarse = cout[...].astype(F32)
    for q in range(HB // 4):
        cell = coarse[q * IC : (q + 1) * IC, :]
        for s in range(4):
            up[q, 0, pl.ds(s, IC, stride=4), :] = cell[:, :128]
            up[q, 1, pl.ds(s, IC, stride=4), :] = cell[:, 128:]
        grown = jnp.concatenate([up[q, 0], up[q, 1]], axis=-1)
        for t in range(4):
            conv_in[4 * q + t] = (fine[4 * q + t].astype(F32) + grown).astype(BF)
    fill_windows(i, oc, rows, left, right, win)
    for b in range(3):
        shifted[:, :, b * CF : (b + 1) * CF] = win[:, 9 - b : 9 - b + TC, :].astype(BF)

    @pl.when(i == 0)
    def _():
        acc[...] = jnp.zeros_like(acc)

    cells = conv_in[...].reshape(HB * TC, CF).T
    for a in range(3):
        acc[a] += dot(cells, shifted[2 - a : 2 - a + HB].reshape(HB * TC, 3 * CF))

    @pl.when(i == NB - 1)
    def _():
        for out, c in ((keep, core[0]), (send, 1 - core[0])):
            half = pl.ds(pl.multiple_of(c * 128, 128), 128)
            for t in range(TAPS):
                for n in range(2):
                    at = (t % 3) * CF + n * 128
                    out[(2 * t + n) * 128 : (2 * t + n + 1) * 128, :] = acc[t // 3, half, at : at + 128].astype(BF)
            out[TAPS * 256 :, :] = jnp.zeros((LATE - TAPS * 256, 128), BF)


def wgrad_pass(core, fine, cout, oc, rows, left, right):
    return pl.pallas_call(
        wgrad_kernel,
        grid=(NB,),
        in_specs=[
            pl.BlockSpec(memory_space=pltpu.SMEM),
            pl.BlockSpec((HB, TC, CF), lambda i: (i, 0, 0)),
            pl.BlockSpec((HB // 4 * IC, CF), lambda i: (i, 0)),
            whole(TR, TC, CF),
            whole(2, TC, CF),
            whole(SIDE, CF),
            whole(SIDE, CF),
        ],
        out_specs=[
            pl.BlockSpec((HB, TC, CF), lambda i: (i, 0, 0)),
            whole(LATE, 128),
            whole(LATE, 128),
        ],
        out_shape=[
            jax.ShapeDtypeStruct((TR, TC, CF), BF),
            jax.ShapeDtypeStruct((LATE, 128), BF),
            jax.ShapeDtypeStruct((LATE, 128), BF),
        ],
        scratch_shapes=[
            pltpu.VMEM((HB // 4, 2, TC, 128), F32),
            pltpu.VMEM((HB + 2, 48, CF), F32),
            pltpu.VMEM((HB + 2, TC, 3 * CF), BF),
            pltpu.VMEM((3, CF, 3 * CF), F32),
        ],
        compiler_params=params(32),
        cost_estimate=cost(8_000_000_000, 9_000_000),
        name="conv_weight_gradient",
    )(core, fine, cout, oc, rows, left, right)


def conv_kernel(ci, rows, left, right, wconv, out, win, wide):
    i = pl.program_id(0)
    fill_windows(i, ci, rows, left, right, win)
    for b in range(3):
        wide[:, :, b * CF : (b + 1) * CF] = win[:, 7 + b : 7 + b + TC, :].astype(BF)
    total = jnp.zeros((HB * TC, CF), F32)
    for a in range(3):
        total += dot(wide[a : a + HB].reshape(HB * TC, 3 * CF), wconv[a])
    out[...] = total.astype(BF).reshape(HB, TC, CF)


def conv_pass(ci, rows, left, right, wconv):
    return pl.pallas_call(
        conv_kernel,
        grid=(NB,),
        in_specs=[
            whole(TR, TC, CF),
            whole(2, TC, CF),
            whole(SIDE, CF),
            whole(SIDE, CF),
            whole(3, 3 * CF, CF),
        ],
        out_specs=pl.BlockSpec((HB, TC, CF), lambda i: (i, 0, 0)),
        out_shape=jax.ShapeDtypeStruct((TR, TC, CF), BF),
        scratch_shapes=[pltpu.VMEM((HB + 2, 48, CF), F32), pltpu.VMEM((HB + 2, TC, 3 * CF), BF)],
        compiler_params=params(32),
        cost_estimate=cost(8_000_000_000, 6_000_000),
        name="conv_forward",
    )(ci, rows, left, right, wconv.reshape(3, 3 * CF, CF))


def add_late_kernel(keep, got, packed, out):
    out[...] = (keep[...].astype(F32) + got[...].astype(F32)).astype(BF)


def add_late(keep, got, packed):
    return pl.pallas_call(
        add_late_kernel,
        grid=(1,),
        in_specs=[whole(LATE, 128), whole(LATE, 128), pl.BlockSpec(memory_space=pl.ANY)],
        out_specs=whole(LATE, 128),
        out_shape=jax.ShapeDtypeStruct((PACK, 128), BF),
        input_output_aliases={2: 0},
        compiler_params=params(16),
        name="late_core_sum",
    )(keep, got, packed)


def place_kernel(core, half, *refs):
    conv, band, point, proj = refs[-4:]

    def place(out, n, start, cols):
        out[:, cols : cols + 128] = half[start : start + n, :].astype(F32)

    for t in range(TAPS):
        for n in range(2):
            place(conv.at[t], 128, (2 * t + n) * 128, 128 * n)
    for k in range(5):
        for n in range(4):
            place(band.at[k] if k < BANDS else point, 256, LATE + (4 * k + n) * 256, 128 * n)
    for n in range(2):
        place(proj, 256, LATE + (20 + n) * 256, 128 * n)


def place_half(core, half, before=()):
    any_ref = pl.BlockSpec(memory_space=pl.ANY)
    return pl.pallas_call(
        place_kernel,
        grid_spec=pltpu.PrefetchScalarGridSpec(
            num_scalar_prefetch=1,
            grid=(1,),
            in_specs=[pl.BlockSpec((PACK, 128), lambda i, c: (0, 0))] + [any_ref] * len(before),
            out_specs=[
                pl.BlockSpec((TAPS, 128, CF), lambda i, c: (0, c[0], 0)),
                pl.BlockSpec((BANDS, 256, C), lambda i, c: (0, c[0], 0)),
                pl.BlockSpec((256, C), lambda i, c: (c[0], 0)),
                pl.BlockSpec((256, CF), lambda i, c: (c[0], 0)),
            ],
        ),
        out_shape=[
            jax.ShapeDtypeStruct((TAPS, CF, CF), F32),
            jax.ShapeDtypeStruct((BANDS, C, C), F32),
            jax.ShapeDtypeStruct((C, C), F32),
            jax.ShapeDtypeStruct((C, CF), F32),
        ],
        input_output_aliases={2 + n: n for n in range(len(before))},
        compiler_params=params(24),
        cost_estimate=cost(0, 6_000_000),
        name="place_gradients",
    )(core, half, *before)


def neighbours(axes, count):
    forward = [(i, i + 1) for i in range(count - 1)]
    return forward, [(b, a) for a, b in forward]


def halo(tile, east_edge, west_edge):
    forward, backward = neighbours(COL, 16)
    west = lax.ppermute(east_edge, COL, forward)
    east = lax.ppermute(west_edge, COL, backward)
    forward, backward = neighbours(ROW, 8)
    low = jnp.concatenate([tile[TR - 1], west[TR - 1 :], east[TR - 1 :]], axis=0)
    high = jnp.concatenate([tile[0], west[:1], east[:1]], axis=0)
    above = lax.ppermute(low, ROW, forward)
    below = lax.ppermute(high, ROW, backward)
    pad = jnp.zeros((SIDE - TR - 2, CF), BF)
    left = jnp.concatenate([above[TC : TC + 1], west, below[TC : TC + 1], pad], axis=0)
    right = jnp.concatenate([above[TC + 1 :], east, below[TC + 1 :], pad], axis=0)
    return jnp.stack([above[:TC], below[:TC]]), left.astype(F32), right.astype(F32)


def local(coarse_in, fine_in, band_weight, point_weight, proj_weight, conv_weight, out_cot):
    core = lax.axis_index("c").astype(jnp.int32).reshape(1)
    swap = [(0, 1), (1, 0)]
    haar = jnp.asarray(haar_matrix(), BF)

    chunks = coarse_in.reshape(2, 8, 16, C).transpose(1, 0, 2, 3)
    chunks = jnp.broadcast_to(chunks[:, None], (8, 2, 2, 16, C)).reshape(16, 2, 16, C)
    chunks, last, first = lax.optimization_barrier((chunks, out_cot[:, TC - 1], out_cot[:, 0]))
    x = lax.all_to_all(chunks, COL, 0, 0, tiled=True).reshape(PAIR, C)
    cot_halo = halo(out_cot, last, first)
    sub, pre, hidden, cout = coarse_pass(core, x, haar, band_weight, point_weight, proj_weight)
    dco = dcoarse_pass(out_cot, *cot_halo, conv_weight)
    dtwin = lax.ppermute(dco, "c", swap)
    conv_in, keep, send = wgrad_pass(core, fine_in, cout, out_cot, *cot_halo)
    got = lax.ppermute(send, "c", swap)
    packed = grads_pass(core, x, haar, proj_weight, sub, pre, hidden, dco, dtwin)
    packed = add_late(keep, got, packed)

    packed, conv_in = lax.optimization_barrier((packed, conv_in))
    parts = lax.all_to_all(packed, CHIPS, 0, 0, tiled=True)
    fine_out = conv_pass(conv_in, *halo(conv_in, conv_in[:, TC - 1], conv_in[:, 0]), conv_weight)
    parts, fine_out = lax.optimization_barrier((parts, fine_out))
    parts = parts.reshape(PEERS, PACK // PEERS, 128)
    done = (jnp.sum(parts.astype(F32), axis=0) * SCALE).astype(BF)
    spread = jnp.broadcast_to(done[None], (PEERS, PACK // PEERS, 128)).reshape(PACK, 128)
    mine = lax.all_to_all(spread, CHIPS, 0, 0, tiled=True)
    other = lax.ppermute(mine, "c", swap)
    grads = place_half(core, mine)
    grad_conv, grad_band, grad_point, grad_proj = place_half(1 - core, other, grads)
    return fine_out, grad_conv, grad_band, grad_point, grad_proj


def solution(mesh):
    fine_mesh = Mesh(
        np.asarray(mesh.devices).reshape([n for _, n in GRID]), tuple(name for name, _ in GRID)
    )
    fine = P(ROW, COL, None)
    in_specs = (P(ROW + COL, None, None), fine, P(), P(), P(), P(), fine)
    out_specs = (fine, P(), P(), P(), P())
    return jax.shard_map(local, mesh=fine_mesh, in_specs=in_specs, out_specs=out_specs, check_vma=False)
```

```python
import functools

import jax
import jax.numpy as jnp
import numpy as np
from jax import lax
from jax.experimental import pallas as pl
from jax.experimental.pallas import tpu as pltpu
from jax.sharding import Mesh
from jax.sharding import PartitionSpec as P

BF = jnp.bfloat16
F32 = jnp.float32
ROW = ("xl", "z")
COL = ("xh", "y", "c")
CHIPS = ("xl", "z", "xh", "y")
GRID = (("xl", 2), ("z", 4), ("xh", 2), ("y", 4), ("c", 2))

C, CF, BANDS, TAPS = 512, 256, 4, 9
TR, TC = 128, 32
IR, IC = 32, 8
CELLS = IR * IC
PAIR = 2 * CELLS
HB = 32
NB = TR // HB
SIDE = 136
LATE = TAPS * 2 * 128 + 256
EARLY = 5 * 4 * 256 + 2 * 256
PACK = LATE + EARLY
PEERS = 64
SCALE = float(1024 * 512) ** (-0.5)
MIB = 1024 * 1024
GELU_A = 0.7978845608028654
GELU_B = 0.044715


def params(mib, grid=1):
    return pltpu.CompilerParams(
        vmem_limit_bytes=mib * MIB, dimension_semantics=("arbitrary",) * grid if grid else None
    )


def cost(flops, moved):
    return pl.CostEstimate(flops=flops, bytes_accessed=moved, transcendentals=0)


def whole(*shape):
    return pl.BlockSpec(shape, lambda i: (0,) * len(shape))


def dot(a, b, dims=((1,), (0,))):
    return lax.dot_general(a, b, (dims, ((), ())), preferred_element_type=F32)


def haar_matrix():
    out = np.zeros((BANDS, 8, 8, 16, 16), np.float32)
    signs = ((1, 1, 1, 1), (1, -1, 1, -1), (1, 1, -1, -1), (1, -1, -1, 1))
    for k in range(BANDS):
        for i in range(8):
            for j in range(8):
                for t in range(4):
                    out[k, i, j, 2 * i + t // 2, 2 * j + t % 2] = 0.5 * signs[k][t]
    return out.reshape(256, 256)


def pool_matrices():
    inner = np.zeros((3, 3, IC, 6, TC), np.float32)
    side = np.zeros((3, IR, SIDE), np.float32)
    for a in range(3):
        for b in range(3):
            for j in range(IC):
                low, high = max(4 * j - b + 1, 0), min(4 * j - b + 4, TC - 1)
                inner[a, b, j, 2 - a : 6 - a, low : high + 1] = 1
        for i in range(IR):
            side[a, i, 4 * i + 2 - a : 4 * i + 6 - a] = 1
    return inner.reshape(TAPS * IC, 6 * TC), side.reshape(3 * IR, SIDE)


def dcoarse_kernel(oc, rows, left, right, inner, side, wconv, out, pooled):
    pool = inner[...]
    for i in range(IR):
        if i == 0:
            block = jnp.concatenate([rows[0], oc[: 5 * TC, :]], axis=0)
        elif i == IR - 1:
            block = jnp.concatenate([oc[(4 * i - 1) * TC :, :], rows[1]], axis=0)
        else:
            block = oc[(4 * i - 1) * TC : (4 * i + 5) * TC, :]
        part = dot(pool, block)
        for t in range(TAPS):
            for h in range(2):
                pooled[t, h, i * IC : (i + 1) * IC, :] = part[t * IC : (t + 1) * IC, h * 128 : (h + 1) * 128]
    for edge, b, start in ((left, 2, 0), (right, 0, IC - 1)):
        part = dot(side[...], edge[...].astype(BF))
        for a in range(3):
            for h in range(2):
                cells = pl.ds(start, IR, stride=IC)
                pooled[3 * a + b, h, cells, :] += part[a * IR : (a + 1) * IR, h * 128 : (h + 1) * 128]
    total = jnp.zeros((CELLS, CF), F32)
    for t in range(TAPS):
        s = jnp.concatenate([pooled[t, 0], pooled[t, 1]], axis=-1).astype(BF)
        total += dot(s, wconv[t], ((1,), (1,)))
    out[...] = total.astype(BF)


def dcoarse_pass(oc, rows, left, right, wconv):
    inner, side = pool_matrices()
    vm = pl.BlockSpec(memory_space=pltpu.VMEM)
    return pl.pallas_call(
        dcoarse_kernel,
        in_specs=[vm] * 7,
        out_specs=vm,
        out_shape=jax.ShapeDtypeStruct((CELLS, CF), BF),
        scratch_shapes=[pltpu.VMEM((TAPS, 2, CELLS, 128), F32)],
        compiler_params=params(16, 0),
        cost_estimate=cost(600_000_000, 4_000_000),
        name="coarse_cotangent",
    )(oc.reshape(TR * TC, CF), rows, left, right, jnp.asarray(inner, BF), jnp.asarray(side, BF), wconv)


def coarse_kernel(core, x, haar, wband, wp_hbm, wj_hbm, sub, pre, hidden, cout, split, outs, wpoint, wproj, sems):
    k = pl.program_id(0)
    loads = [
        pltpu.make_async_copy(src, dst, sems.at[n])
        for n, (src, dst) in enumerate(((wp_hbm, wpoint), (wj_hbm, wproj)))
    ]

    @pl.when(k == 0)
    def _():
        for load in loads:
            load.start()

    h = haar[pl.ds(pl.multiple_of(k * 64, 64), 64), :]
    part = jnp.concatenate([dot(h, x[:256, :]), dot(h, x[256:, :])], axis=0).astype(BF)
    sub[pl.ds(pl.multiple_of(k * 128, 128), 128), :] = part
    m = dot(part, wband[0])
    hi = m.astype(BF)
    lo = (m - hi.astype(F32)).astype(BF)
    rows = pl.ds(pl.multiple_of(k * 64, 64), 64)
    for g in range(2):
        split[g, 0, rows, :] = hi[g * 64 : (g + 1) * 64]
        split[g, 1, rows, :] = lo[g * 64 : (g + 1) * 64]

    @pl.when(k == BANDS - 1)
    def _():
        for load in loads:
            load.wait()
        h = haar[...]
        for g in range(2):
            cells = slice(g * 256, (g + 1) * 256)
            value = dot(h, split[g, 0], ((0,), (0,))) + dot(h, split[g, 1], ((0,), (0,)))
            value = value + dot(x[cells, :], wpoint[...])
            pre[cells, :] = value
            act = 0.5 * value * (1.0 + jnp.tanh(GELU_A * (value + GELU_B * (value * value * value))))
            act = act.astype(BF)
            hidden[cells, :] = act
            outs[g * 16 : (g + 1) * 16] = dot(act, wproj[...]).reshape(16, 16, CF)
        own = outs[:, pl.ds(pl.multiple_of(core[0] * IC, IC), IC), :]
        cout[...] = own.reshape(CELLS, CF).astype(BF)


def coarse_pass(core, x, haar, wband, wpoint, wproj):
    return pl.pallas_call(
        coarse_kernel,
        grid=(BANDS,),
        in_specs=[
            pl.BlockSpec(memory_space=pltpu.SMEM),
            whole(PAIR, C),
            whole(256, 256),
            pl.BlockSpec((1, C, C), lambda i: (i, 0, 0)),
            pl.BlockSpec(memory_space=pl.ANY),
            pl.BlockSpec(memory_space=pl.ANY),
        ],
        out_specs=[whole(PAIR, C), whole(PAIR, C), whole(PAIR, C), whole(CELLS, CF)],
        out_shape=[
            jax.ShapeDtypeStruct((PAIR, C), BF),
            jax.ShapeDtypeStruct((PAIR, C), F32),
            jax.ShapeDtypeStruct((PAIR, C), BF),
            jax.ShapeDtypeStruct((CELLS, CF), BF),
        ],
        scratch_shapes=[
            pltpu.VMEM((2, 2, 256, C), BF),
            pltpu.VMEM((IR, 2 * IC, CF), F32),
            pltpu.VMEM((C, C), BF),
            pltpu.VMEM((C, CF), BF),
            pltpu.SemaphoreType.DMA((2,)),
        ],
        compiler_params=params(16),
        cost_estimate=cost(1_000_000_000, 6_000_000),
        name="coarse_forward",
    )(core, x, haar, wband, wpoint, wproj)


def grads_kernel(core, x_hbm, haar, wproj, sub_hbm, pre, hidden_hbm, dco, dtwin, out, both, x, sub, hidden, sems):
    loads = [
        pltpu.make_async_copy(src, dst, sems.at[n])
        for n, (src, dst) in enumerate(((sub_hbm, sub), (x_hbm, x), (hidden_hbm, hidden)))
    ]
    for load in loads:
        load.start()
    own = pl.multiple_of(core[0] * IC, IC)
    both[:, pl.ds(own, IC), :] = dco[...].astype(F32).reshape(IR, IC, CF)
    both[:, pl.ds(IC - own, IC), :] = dtwin[...].astype(F32).reshape(IR, IC, CF)
    d = both[...].reshape(PAIR, CF).astype(BF)
    value = pre[...]
    square = value * value
    th = jnp.tanh(GELU_A * (value + GELU_B * (value * square)))
    slope = 0.5 * (1.0 + th) + 0.5 * value * (1.0 - th * th) * (GELU_A * (1.0 + 3.0 * GELU_B * square))
    dpre = (dot(d, wproj[...], ((1,), (1,))) * slope).astype(BF)
    h = haar[...]
    dmix = [dot(h, dpre[g * 256 : (g + 1) * 256]).astype(BF) for g in range(2)]
    half = pl.ds(pl.multiple_of(core[0] * 256, 256), 256)
    for load in loads:
        load.wait()
    for k in range(5):
        if k < BANDS:
            dk = jnp.concatenate([dmix[g][k * 64 : (k + 1) * 64] for g in range(2)], axis=0)
            grad = dot(sub[k * 128 : (k + 1) * 128, half], dk, ((0,), (0,)))
        else:
            grad = dot(x[:, half], dpre, ((0,), (0,)))
        for n in range(4):
            at = LATE + (4 * k + n) * 256
            out[at : at + 256, :] = grad[:, n * 128 : (n + 1) * 128].astype(BF)
    grad = dot(hidden[:, half], d, ((0,), (0,)))
    for n in range(2):
        at = LATE + (20 + n) * 256
        out[at : at + 256, :] = grad[:, n * 128 : (n + 1) * 128].astype(BF)


def grads_pass(core, x, haar, wproj, sub, pre, hidden, dco, dtwin):
    vm, hbm = pl.BlockSpec(memory_space=pltpu.VMEM), pl.BlockSpec(memory_space=pl.ANY)
    return pl.pallas_call(
        grads_kernel,
        in_specs=[pl.BlockSpec(memory_space=pltpu.SMEM), hbm, vm, vm, hbm, vm, hbm, vm, vm],
        out_specs=vm,
        out_shape=jax.ShapeDtypeStruct((PACK, 128), BF),
        scratch_shapes=[pltpu.VMEM((IR, 2 * IC, CF), F32)]
        + [pltpu.VMEM((PAIR, C), BF)] * 3
        + [pltpu.SemaphoreType.DMA((3,))],
        compiler_params=params(16, 0),
        cost_estimate=cost(1_000_000_000, 6_000_000),
        name="coarse_gradients",
    )(core, x, haar, wproj, sub, pre, hidden, dco, dtwin)


def window_specs():
    return [
        pl.BlockSpec((1, TC, CF), lambda i: (jnp.maximum(i * HB - 1, 0), 0, 0)),
        pl.BlockSpec((HB, TC, CF), lambda i: (i, 0, 0)),
        pl.BlockSpec((1, TC, CF), lambda i: (jnp.minimum(i * HB + HB, TR - 1), 0, 0)),
        whole(2, TC, CF),
        whole(SIDE, CF),
        whole(SIDE, CF),
    ]


def fill_windows(i, before, tile, after, rows, left, right, win):
    r0 = i * HB
    win[1 : HB + 1, 8 : 8 + TC, :] = tile[...].astype(F32)
    win[0:1, 8 : 8 + TC, :] = jnp.where(i == 0, rows[0:1], before[...]).astype(F32)
    win[HB + 1 : HB + 2, 8 : 8 + TC, :] = jnp.where(i == NB - 1, rows[1:2], after[...]).astype(F32)
    for r in range(HB + 2):
        win[r, 7:8, :] = left[pl.ds(r0 + r, 1), :]
        win[r, 8 + TC : 9 + TC, :] = right[pl.ds(r0 + r, 1), :]


def wgrad_kernel(
    core, fine, cout, before, oc, after, rows, left, right, conv_in, keep, send, up, win, shifted, acc
):
    i = pl.program_id(0)
    coarse = cout[...].astype(F32)
    for q in range(HB // 4):
        cell = coarse[q * IC : (q + 1) * IC, :]
        for s in range(4):
            up[q, 0, pl.ds(s, IC, stride=4), :] = cell[:, :128]
            up[q, 1, pl.ds(s, IC, stride=4), :] = cell[:, 128:]
        grown = jnp.concatenate([up[q, 0], up[q, 1]], axis=-1)
        for t in range(4):
            conv_in[4 * q + t] = (fine[4 * q + t].astype(F32) + grown).astype(BF)
    fill_windows(i, before, oc, after, rows, left, right, win)
    for b in range(3):
        shifted[:, :, b * CF : (b + 1) * CF] = win[:, 9 - b : 9 - b + TC, :].astype(BF)

    @pl.when(i == 0)
    def _():
        acc[...] = jnp.zeros_like(acc)

    cells = conv_in[...].reshape(HB * TC, CF).T
    for a in range(3):
        acc[a] += dot(cells, shifted[2 - a : 2 - a + HB].reshape(HB * TC, 3 * CF))

    @pl.when(i == NB - 1)
    def _():
        for out, c in ((keep, core[0]), (send, 1 - core[0])):
            half = pl.ds(pl.multiple_of(c * 128, 128), 128)
            for t in range(TAPS):
                for n in range(2):
                    at = (t % 3) * CF + n * 128
                    out[(2 * t + n) * 128 : (2 * t + n + 1) * 128, :] = acc[t // 3, half, at : at + 128].astype(BF)
            out[TAPS * 256 :, :] = jnp.zeros((LATE - TAPS * 256, 128), BF)


def wgrad_pass(core, fine, cout, oc, rows, left, right):
    return pl.pallas_call(
        wgrad_kernel,
        grid=(NB,),
        in_specs=[
            pl.BlockSpec(memory_space=pltpu.SMEM),
            pl.BlockSpec((HB, TC, CF), lambda i: (i, 0, 0)),
            pl.BlockSpec((HB // 4 * IC, CF), lambda i: (i, 0)),
        ]
        + window_specs(),
        out_specs=[
            pl.BlockSpec((HB, TC, CF), lambda i: (i, 0, 0)),
            whole(LATE, 128),
            whole(LATE, 128),
        ],
        out_shape=[
            jax.ShapeDtypeStruct((TR, TC, CF), BF),
            jax.ShapeDtypeStruct((LATE, 128), BF),
            jax.ShapeDtypeStruct((LATE, 128), BF),
        ],
        scratch_shapes=[
            pltpu.VMEM((HB // 4, 2, TC, 128), F32),
            pltpu.VMEM((HB + 2, 48, CF), F32),
            pltpu.VMEM((HB + 2, TC, 3 * CF), BF),
            pltpu.VMEM((3, CF, 3 * CF), F32),
        ],
        compiler_params=params(16),
        cost_estimate=cost(8_000_000_000, 9_000_000),
        name="conv_weight_gradient",
    )(core, fine, cout, oc, oc, oc, rows, left, right)


def conv_kernel(before, ci, after, rows, left, right, wconv, out, win, wide):
    i = pl.program_id(0)
    fill_windows(i, before, ci, after, rows, left, right, win)
    for b in range(3):
        wide[:, :, b * CF : (b + 1) * CF] = win[:, 7 + b : 7 + b + TC, :].astype(BF)
    total = jnp.zeros((HB * TC, CF), F32)
    for a in range(3):
        total += dot(wide[a : a + HB].reshape(HB * TC, 3 * CF), wconv[a])
    out[...] = total.astype(BF).reshape(HB, TC, CF)


def conv_pass(ci, rows, left, right, wconv):
    return pl.pallas_call(
        conv_kernel,
        grid=(NB,),
        in_specs=window_specs() + [whole(3, 3 * CF, CF)],
        out_specs=pl.BlockSpec((HB, TC, CF), lambda i: (i, 0, 0)),
        out_shape=jax.ShapeDtypeStruct((TR, TC, CF), BF),
        scratch_shapes=[pltpu.VMEM((HB + 2, 48, CF), F32), pltpu.VMEM((HB + 2, TC, 3 * CF), BF)],
        compiler_params=params(16),
        cost_estimate=cost(1_000_000, 1_000_000),
        name="conv_forward",
    )(ci, ci, ci, rows, left, right, wconv.reshape(3, 3 * CF, CF))


def add_late_kernel(keep, got, packed, out):
    out[...] = (keep[...].astype(F32) + got[...].astype(F32)).astype(BF)


def add_late(keep, got, packed):
    return pl.pallas_call(
        add_late_kernel,
        grid=(1,),
        in_specs=[whole(LATE, 128), whole(LATE, 128), pl.BlockSpec(memory_space=pl.ANY)],
        out_specs=whole(LATE, 128),
        out_shape=jax.ShapeDtypeStruct((PACK, 128), BF),
        input_output_aliases={2: 0},
        compiler_params=params(16),
        name="late_core_sum",
    )(keep, got, packed)


def place_kernel(core, half, *refs):
    conv, band, point, proj = refs[-4:]

    def place(out, n, start, cols):
        out[:, cols : cols + 128] = half[start : start + n, :].astype(F32)

    for t in range(TAPS):
        for n in range(2):
            place(conv.at[t], 128, (2 * t + n) * 128, 128 * n)
    for k in range(5):
        for n in range(4):
            place(band.at[k] if k < BANDS else point, 256, LATE + (4 * k + n) * 256, 128 * n)
    for n in range(2):
        place(proj, 256, LATE + (20 + n) * 256, 128 * n)


def place_half(core, half, before=()):
    any_ref = pl.BlockSpec(memory_space=pl.ANY)
    return pl.pallas_call(
        place_kernel,
        grid_spec=pltpu.PrefetchScalarGridSpec(
            num_scalar_prefetch=1,
            grid=(1,),
            in_specs=[pl.BlockSpec((PACK, 128), lambda i, c: (0, 0))] + [any_ref] * len(before),
            out_specs=[
                pl.BlockSpec((TAPS, 128, CF), lambda i, c: (0, c[0], 0)),
                pl.BlockSpec((BANDS, 256, C), lambda i, c: (0, c[0], 0)),
                pl.BlockSpec((256, C), lambda i, c: (c[0], 0)),
                pl.BlockSpec((256, CF), lambda i, c: (c[0], 0)),
            ],
        ),
        out_shape=[
            jax.ShapeDtypeStruct((TAPS, CF, CF), F32),
            jax.ShapeDtypeStruct((BANDS, C, C), F32),
            jax.ShapeDtypeStruct((C, C), F32),
            jax.ShapeDtypeStruct((C, CF), F32),
        ],
        input_output_aliases={2 + n: n for n in range(len(before))},
        compiler_params=params(16),
        cost_estimate=cost(0, 6_000_000),
        name="place_gradients",
    )(core, half, *before)


def shift(value, axes, count, step):
    pairs = [(i, i + step) for i in range(count) if 0 <= i + step < count]
    return lax.ppermute(value, axes, pairs)


def side_edges(first, last):
    lower = lax.axis_index("c") == 0
    twin = lax.ppermute(jnp.where(lower, last, first), "c", [(0, 1), (1, 0)])
    pairs = [(2 * k + 1, 2 * k + 2) for k in range(7)]
    pairs = pairs + [(b, a) for a, b in pairs]
    chip = lax.ppermute(jnp.where(lower, first, last), COL, pairs)
    return jnp.where(lower, chip, twin), jnp.where(lower, twin, chip)


def sides(corners, west, east):
    pad = jnp.zeros((SIDE - TR - 2, CF), BF)
    left = jnp.concatenate([corners[0], west, corners[2], pad], axis=0)
    right = jnp.concatenate([corners[1], east, corners[3], pad], axis=0)
    return left.astype(F32), right.astype(F32)


def row_halo(tile, west, east):
    low = jnp.concatenate([tile[TR - 1], west[TR - 1 :], east[TR - 1 :]], axis=0)
    high = jnp.concatenate([tile[0], west[:1], east[:1]], axis=0)
    above, below = shift(low, ROW, 8, 1), shift(high, ROW, 8, -1)
    corners = [part for row in (above, below) for part in (row[TC : TC + 1], row[TC + 1 :])]
    return (jnp.stack([above[:TC], below[:TC]]),) + sides(corners, west, east)


def whole_halo(tile):
    first, last = tile[:, 0], tile[:, TC - 1]
    lower = lax.axis_index("c") == 0
    inner, outer = jnp.where(lower, last, first), jnp.where(lower, first, last)
    twin = lax.ppermute(inner, "c", [(0, 1), (1, 0)])
    chips = [(2 * k + 1, 2 * k + 2) for k in range(7)]
    chips = chips + [(b, a) for a, b in chips]
    chip = lax.ppermute(outer, COL, chips)
    rows, far = [], []
    for down, at in ((1, TR - 1), (-1, 0)):
        rows.append(shift(jnp.concatenate([tile[at], twin[at : at + 1]], axis=0), ROW, 8, down))
        pairs = [(16 * r + a, 16 * (r + down) + b) for r in range(8) for a, b in chips if 0 <= r + down < 8]
        far.append(lax.ppermute(outer[at : at + 1], ROW + COL, pairs))
    west, east = jnp.where(lower, chip, twin), jnp.where(lower, twin, chip)
    corners = []
    for row, cell in zip(rows, far):
        near = row[TC:]
        corners += [jnp.where(lower, cell, near), jnp.where(lower, near, cell)]
    return (jnp.stack([row[:TC] for row in rows]),) + sides(corners, west, east)


def local(coarse_in, fine_in, band_weight, point_weight, proj_weight, conv_weight, out_cot):
    core = lax.axis_index("c").astype(jnp.int32).reshape(1)
    swap = [(0, 1), (1, 0)]
    haar = jnp.asarray(haar_matrix(), BF)

    chunks = coarse_in.reshape(2, 8, 16, C).transpose(1, 0, 2, 3)
    chunks = jnp.broadcast_to(chunks[:, None], (8, 2, 2, 16, C)).reshape(16, 2, 16, C)
    west, east = side_edges(out_cot[:, 0], out_cot[:, TC - 1])
    chunks, west, east = lax.optimization_barrier((chunks, west, east))
    cot_halo = row_halo(out_cot, west, east)
    x = lax.all_to_all(chunks, COL, 0, 0, tiled=True).reshape(PAIR, C)
    dco = dcoarse_pass(out_cot, *cot_halo, conv_weight)
    dtwin = lax.ppermute(dco, "c", swap)
    x, dtwin = lax.optimization_barrier((x, dtwin))
    sub, pre, hidden, cout = coarse_pass(core, x, haar, band_weight, point_weight, proj_weight)
    conv_in, keep, send = wgrad_pass(core, fine_in, cout, out_cot, *cot_halo)
    got = lax.ppermute(send, "c", swap)
    packed = grads_pass(core, x, haar, proj_weight, sub, pre, hidden, dco, dtwin)
    packed = add_late(keep, got, packed)

    packed, conv_in = lax.optimization_barrier((packed, conv_in))
    parts = lax.all_to_all(packed, CHIPS, 0, 0, tiled=True)
    conv_halo = whole_halo(conv_in)
    parts = parts.reshape(PEERS, PACK // PEERS, 128)
    done = (jnp.sum(parts.astype(F32), axis=0) * SCALE).astype(BF)
    spread = jnp.broadcast_to(done[None], (PEERS, PACK // PEERS, 128)).reshape(PACK, 128)
    spread, conv_halo = lax.optimization_barrier((spread, conv_halo))
    mine = lax.all_to_all(spread, CHIPS, 0, 0, tiled=True)
    fine_out = conv_pass(conv_in, *conv_halo, conv_weight)
    mine, fine_out = lax.optimization_barrier((mine, fine_out))
    other = lax.ppermute(mine, "c", swap)
    grads = place_half(core, mine)
    grad_conv, grad_band, grad_point, grad_proj = place_half(1 - core, other, grads)
    return fine_out, grad_conv, grad_band, grad_point, grad_proj


def solution(mesh):
    fine_mesh = Mesh(
        np.asarray(mesh.devices).reshape([n for _, n in GRID]), tuple(name for name, _ in GRID)
    )
    fine = P(ROW, COL, None)
    in_specs = (P(ROW + COL, None, None), fine, P(), P(), P(), P(), fine)
    out_specs = (fine, P(), P(), P(), P())
    return jax.shard_map(local, mesh=fine_mesh, in_specs=in_specs, out_specs=out_specs, check_vma=False)
```

```python
import functools

import jax
import jax.numpy as jnp
import numpy as np
from jax import lax
from jax.experimental import pallas as pl
from jax.experimental.pallas import tpu as pltpu
from jax.sharding import Mesh
from jax.sharding import PartitionSpec as P

BF = jnp.bfloat16
F32 = jnp.float32
ROW = ("xl", "z")
COL = ("xh", "y", "c")
CHIPS = ("xl", "z", "xh", "y")
GRID = (("xl", 2), ("z", 4), ("xh", 2), ("y", 4), ("c", 2))

C, CF, BANDS, TAPS = 512, 256, 4, 9
TR, TC = 128, 32
IR, IC = 32, 8
CELLS = IR * IC
PAIR = 2 * CELLS
HB = 32
NB = TR // HB
SIDE = 136
LATE = TAPS * 2 * 128 + 256
EARLY = 5 * 4 * 256 + 2 * 256
PACK = LATE + EARLY
PEERS = 64
SCALE = float(1024 * 512) ** (-0.5)
MIB = 1024 * 1024
GELU_A = 0.7978845608028654
GELU_B = 0.044715


def params(mib, grid=1):
    return pltpu.CompilerParams(
        vmem_limit_bytes=mib * MIB, dimension_semantics=("arbitrary",) * grid if grid else None
    )


def cost(flops, moved):
    return pl.CostEstimate(flops=flops, bytes_accessed=moved, transcendentals=0)


def whole(*shape):
    return pl.BlockSpec(shape, lambda i: (0,) * len(shape))


def dot(a, b, dims=((1,), (0,))):
    return lax.dot_general(a, b, (dims, ((), ())), preferred_element_type=F32)


def iotas(*shape):
    return tuple(lax.broadcasted_iota(jnp.int32, shape, n) for n in range(len(shape)))


def haar_matrix():
    row, col = iotas(256, 256)
    inside = ((row >> 3) & 7 == col >> 5) & (row & 7 == (col & 15) >> 1)
    flip = ((row >> 6) & col & 1) ^ ((row >> 7) & (col >> 4) & 1)
    return jnp.where(inside, 0.5 - flip.astype(F32), 0.0).astype(BF)


def pool_matrix():
    row, col = iotas(TAPS * IC, 6 * TC)
    tap, j = row >> 3, row & 7
    a = (tap >= 3).astype(jnp.int32) + (tap >= 6).astype(jnp.int32)
    u = (col >> 5) + a - 2
    v = (col & 31) + (tap - 3 * a) - 1 - 4 * j
    return ((u >= 0) & (u < 4) & (v >= 0) & (v < 4)).astype(F32).astype(BF)


def side_matrix():
    row, col = iotas(3 * IR, SIDE)
    u = col + (row >> 5) - 2 - 4 * (row & 31)
    return ((u >= 0) & (u < 4)).astype(F32).astype(BF)


def dcoarse_kernel(oc, rows, left, right, wconv, out, pooled):
    pool, side = pool_matrix(), side_matrix()
    for i in range(IR):
        if i == 0:
            block = jnp.concatenate([rows[0], oc[: 5 * TC, :]], axis=0)
        elif i == IR - 1:
            block = jnp.concatenate([oc[(4 * i - 1) * TC :, :], rows[1]], axis=0)
        else:
            block = oc[(4 * i - 1) * TC : (4 * i + 5) * TC, :]
        part = dot(pool, block)
        for t in range(TAPS):
            for h in range(2):
                pooled[t, h, i * IC : (i + 1) * IC, :] = part[t * IC : (t + 1) * IC, h * 128 : (h + 1) * 128]
    for edge, b, start in ((left, 2, 0), (right, 0, IC - 1)):
        part = dot(side, edge[...].astype(BF))
        for a in range(3):
            for h in range(2):
                cells = pl.ds(start, IR, stride=IC)
                pooled[3 * a + b, h, cells, :] += part[a * IR : (a + 1) * IR, h * 128 : (h + 1) * 128]
    total = jnp.zeros((CELLS, CF), F32)
    for t in range(TAPS):
        s = jnp.concatenate([pooled[t, 0], pooled[t, 1]], axis=-1).astype(BF)
        total += dot(s, wconv[t], ((1,), (1,)))
    out[...] = total.astype(BF)


def dcoarse_pass(oc, rows, left, right, wconv):
    vm = pl.BlockSpec(memory_space=pltpu.VMEM)
    return pl.pallas_call(
        dcoarse_kernel,
        in_specs=[vm] * 5,
        out_specs=vm,
        out_shape=jax.ShapeDtypeStruct((CELLS, CF), BF),
        scratch_shapes=[pltpu.VMEM((TAPS, 2, CELLS, 128), F32)],
        compiler_params=params(16, 0),
        cost_estimate=cost(1_000, 1_000),
        name="coarse_cotangent",
    )(oc.reshape(TR * TC, CF), rows, left, right, wconv)


def coarse_gradients(core, haar, x, wproj, sub, slope, hidden, dco, dtwin, out, both):
    own = pl.multiple_of(core[0] * IC, IC)
    both[:, pl.ds(own, IC), :] = dco[...].astype(F32).reshape(IR, IC, CF)
    both[:, pl.ds(IC - own, IC), :] = dtwin[...].astype(F32).reshape(IR, IC, CF)
    d = both[...].reshape(PAIR, CF).astype(BF)
    dpre = (dot(d, wproj[...], ((1,), (1,))) * slope[...]).astype(BF)
    dmix = [dot(haar, dpre[g * 256 : (g + 1) * 256]).astype(BF) for g in range(2)]
    half = pl.ds(pl.multiple_of(core[0] * 256, 256), 256)
    for k in range(5):
        if k < BANDS:
            dk = jnp.concatenate([dmix[g][k * 64 : (k + 1) * 64] for g in range(2)], axis=0)
            grad = dot(sub[k * 128 : (k + 1) * 128, half], dk, ((0,), (0,)))
        else:
            grad = dot(x[:, half], dpre, ((0,), (0,)))
        for n in range(4):
            out[(4 * k + n) * 256 : (4 * k + n + 1) * 256, :] = grad[:, n * 128 : (n + 1) * 128].astype(BF)
    grad = dot(hidden[:, half], d, ((0,), (0,)))
    for n in range(2):
        out[(20 + n) * 256 : (21 + n) * 256, :] = grad[:, n * 128 : (n + 1) * 128].astype(BF)


def forward_kernel(
    core, x_hbm, wb_hbm, wp_hbm, wj_hbm, fine_hbm, oc_hbm, dco, dtwin, rows, left, right,
    packed, conv_in, edges, keep, send,
    x, wband, wpoint, wproj, fine, oc, split, outs, up, ends, win, shifted, acc,
    sub, slope, hidden, early, both, sems,
):
    pairs = [(x_hbm, x)] + [(wb_hbm.at[k], wband.at[k]) for k in range(BANDS)]
    pairs += [(wp_hbm, wpoint), (wj_hbm, wproj), (fine_hbm, fine), (oc_hbm, oc)]
    loads = [pltpu.make_async_copy(src, dst, sems.at[n]) for n, (src, dst) in enumerate(pairs)]
    store = pltpu.make_async_copy(early, packed.at[pl.ds(LATE, EARLY)], sems.at[len(pairs)])

    for load in loads:
        load.start()
    haar = haar_matrix()
    loads[0].wait()
    parts = [dot(haar, x[g * 256 : (g + 1) * 256, :]).astype(BF) for g in range(2)]
    for k in range(BANDS):
        part = jnp.concatenate([p[k * 64 : (k + 1) * 64] for p in parts], axis=0)
        sub[k * 128 : (k + 1) * 128, :] = part
        loads[1 + k].wait()
        m = dot(part, wband[k])
        hi = m.astype(BF)
        lo = (m - hi.astype(F32)).astype(BF)
        for g in range(2):
            split[g, 0, k * 64 : (k + 1) * 64, :] = hi[g * 64 : (g + 1) * 64]
            split[g, 1, k * 64 : (k + 1) * 64, :] = lo[g * 64 : (g + 1) * 64]
    loads[5].wait()
    loads[6].wait()
    for g in range(2):
        cells = slice(g * 256, (g + 1) * 256)
        value = dot(haar, split[g, 0], ((0,), (0,))) + dot(haar, split[g, 1], ((0,), (0,)))
        value = value + dot(x[cells, :], wpoint[...])
        square = value * value
        th = jnp.tanh(GELU_A * (value + GELU_B * (value * square)))
        slope[cells, :] = 0.5 * (1.0 + th) + 0.5 * value * (1.0 - th * th) * (GELU_A * (1.0 + 3.0 * GELU_B * square))
        act = (0.5 * value * (1.0 + th)).astype(BF)
        hidden[cells, :] = act
        outs[g * 16 : (g + 1) * 16] = dot(act, wproj[...]).astype(BF).astype(F32).reshape(16, 16, CF)
    coarse_gradients(core, haar, x, wproj, sub, slope, hidden, dco, dtwin, early, both)
    store.start()
    loads[7].wait()
    loads[8].wait()

    def prepare(i):
        r0, slot = i * HB, i % 2
        for q in range(HB // 4):
            cell = outs[r0 // 4 + q, own, :]
            for s in range(4):
                up[slot, q, 0, pl.ds(s, IC, stride=4), :] = cell[:, :128]
                up[slot, q, 1, pl.ds(s, IC, stride=4), :] = cell[:, 128:]
            grown = jnp.concatenate([up[slot, q, 0], up[slot, q, 1]], axis=-1)
            for t in range(4):
                r = r0 + 4 * q + t
                value = fine[r].astype(F32) + grown
                fine[r] = value.astype(BF)
                ends[0, r : r + 1, :] = value[:1]
                ends[1, r : r + 1, :] = value[TC - 1 :]
        before = rows[0:1] if i == 0 else oc[r0 - 1 : r0]
        after = rows[1:2] if i == NB - 1 else oc[r0 + HB : r0 + HB + 1]
        fill_windows(r0, before, oc[r0 : r0 + HB], after, left, right, win.at[slot])
        for b in range(3):
            shifted[slot, :, :, b * CF : (b + 1) * CF] = win[slot, :, 9 - b : 9 - b + TC, :].astype(BF)

    def multiply(i):
        cells = fine[i * HB : (i + 1) * HB].reshape(HB * TC, CF).T
        for a in range(3):
            part = dot(cells, shifted[i % 2, 2 - a : 2 - a + HB].reshape(HB * TC, 3 * CF))
            acc[a] = part if i == 0 else acc[a] + part

    own = pl.ds(pl.multiple_of(core[0] * IC, IC), IC)
    prepare(0)
    for i in range(NB):
        if i + 1 < NB:
            prepare(i + 1)
        multiply(i)
    back = pltpu.make_async_copy(fine, conv_in, sems.at[len(pairs) + 1])
    back.start()
    edges[...] = ends[...].astype(BF)
    for out, c in ((keep, core[0]), (send, 1 - core[0])):
        half = pl.ds(pl.multiple_of(c * 128, 128), 128)
        for t in range(TAPS):
            for n in range(2):
                at = (t % 3) * CF + n * 128
                out[(2 * t + n) * 128 : (2 * t + n + 1) * 128, :] = acc[t // 3, half, at : at + 128].astype(BF)
        out[TAPS * 256 :, :] = jnp.zeros((LATE - TAPS * 256, 128), BF)
    store.wait()
    back.wait()


def forward_pass(core, x, wband, wpoint, wproj, fine, oc, dco, dtwin, rows, left, right):
    hbm, vm = pl.BlockSpec(memory_space=pltpu.HBM), pl.BlockSpec(memory_space=pltpu.VMEM)
    return pl.pallas_call(
        forward_kernel,
        in_specs=[pl.BlockSpec(memory_space=pltpu.SMEM)]
        + [hbm] * 6
        + [vm] * 5,
        out_specs=[hbm, hbm, vm, vm, vm],
        out_shape=[
            jax.ShapeDtypeStruct((PACK, 128), BF),
            jax.ShapeDtypeStruct((TR, TC, CF), BF),
            jax.ShapeDtypeStruct((2, TR, CF), BF),
            jax.ShapeDtypeStruct((LATE, 128), BF),
            jax.ShapeDtypeStruct((LATE, 128), BF),
        ],
        scratch_shapes=[
            pltpu.VMEM((PAIR, C), BF),
            pltpu.VMEM((BANDS, C, C), BF),
            pltpu.VMEM((C, C), BF),
            pltpu.VMEM((C, CF), BF),
            pltpu.VMEM((TR, TC, CF), BF),
            pltpu.VMEM((TR, TC, CF), BF),
            pltpu.VMEM((2, 2, 256, C), BF),
            pltpu.VMEM((IR, 2 * IC, CF), F32),
            pltpu.VMEM((2, HB // 4, 2, TC, 128), F32),
            pltpu.VMEM((2, TR, CF), F32),
            pltpu.VMEM((2, HB + 2, 48, CF), F32),
            pltpu.VMEM((2, HB + 2, TC, 3 * CF), BF),
            pltpu.VMEM((3, CF, 3 * CF), F32),
            pltpu.VMEM((PAIR, C), BF),
            pltpu.VMEM((PAIR, C), F32),
            pltpu.VMEM((PAIR, C), BF),
            pltpu.VMEM((EARLY, 128), BF),
            pltpu.VMEM((IR, 2 * IC, CF), F32),
            pltpu.SemaphoreType.DMA((11,)),
        ],
        compiler_params=params(56, 0),
        cost_estimate=cost(8_000_000_000, 14_000_000),
        name="forward_and_gradients",
    )(core, x, wband, wpoint, wproj, fine, oc, dco, dtwin, rows, left, right)


def window_specs():
    return [
        pl.BlockSpec((1, TC, CF), lambda i: (jnp.maximum(i * HB - 1, 0), 0, 0)),
        pl.BlockSpec((HB, TC, CF), lambda i: (i, 0, 0)),
        pl.BlockSpec((1, TC, CF), lambda i: (jnp.minimum(i * HB + HB, TR - 1), 0, 0)),
        whole(2, TC, CF),
        whole(SIDE, CF),
        whole(SIDE, CF),
    ]


def fill_windows(r0, before, tile, after, left, right, win):
    win[1 : HB + 1, 8 : 8 + TC, :] = tile.astype(F32)
    win[0:1, 8 : 8 + TC, :] = before.astype(F32)
    win[HB + 1 : HB + 2, 8 : 8 + TC, :] = after.astype(F32)
    for r in range(HB + 2):
        win[r, 7:8, :] = left[pl.ds(r0 + r, 1), :]
        win[r, 8 + TC : 9 + TC, :] = right[pl.ds(r0 + r, 1), :]


def conv_kernel(before, ci, after, rows, left, right, wconv, out, win, wide):
    i = pl.program_id(0)
    above = jnp.where(i == 0, rows[0:1], before[...])
    below = jnp.where(i == NB - 1, rows[1:2], after[...])
    fill_windows(i * HB, above, ci[...], below, left, right, win)
    for b in range(3):
        wide[:, :, b * CF : (b + 1) * CF] = win[:, 7 + b : 7 + b + TC, :].astype(BF)
    total = jnp.zeros((HB * TC, CF), F32)
    for a in range(3):
        total += dot(wide[a : a + HB].reshape(HB * TC, 3 * CF), wconv[a])
    out[...] = total.astype(BF).reshape(HB, TC, CF)


def conv_pass(ci, rows, left, right, wconv):
    return pl.pallas_call(
        conv_kernel,
        grid=(NB,),
        in_specs=window_specs() + [whole(3, 3 * CF, CF)],
        out_specs=pl.BlockSpec((HB, TC, CF), lambda i: (i, 0, 0)),
        out_shape=jax.ShapeDtypeStruct((TR, TC, CF), BF),
        scratch_shapes=[pltpu.VMEM((HB + 2, 48, CF), F32), pltpu.VMEM((HB + 2, TC, 3 * CF), BF)],
        compiler_params=params(16),
        cost_estimate=cost(1_000_000, 1_000_000),
        name="conv_forward",
    )(ci, ci, ci, rows, left, right, wconv.reshape(3, 3 * CF, CF))


def reduce_kernel(parts, out, held, copies, sems):
    n = PEERS // 8
    loads = [pltpu.make_async_copy(parts.at[pl.ds(g * n, n)], held.at[g], sems.at[g]) for g in range(8)]
    for load in loads:
        load.start()
    total = None
    for g in range(8):
        loads[g].wait()
        part = jnp.sum(held[g].astype(F32), axis=0)
        total = part if total is None else total + part
    done = (total * SCALE).astype(BF)
    for p in range(n):
        copies[p] = done
    stores = [pltpu.make_async_copy(copies, out.at[pl.ds(g * n, n)], sems.at[8 + g]) for g in range(8)]
    for store in stores:
        store.start()
    for store in stores:
        store.wait()


def reduce_pass(parts):
    n = PACK // PEERS
    hbm = pl.BlockSpec(memory_space=pltpu.HBM)
    return pl.pallas_call(
        reduce_kernel,
        in_specs=[hbm],
        out_specs=hbm,
        out_shape=jax.ShapeDtypeStruct((PEERS, n, 128), BF),
        scratch_shapes=[
            pltpu.VMEM((8, PEERS // 8, n, 128), BF),
            pltpu.VMEM((PEERS // 8, n, 128), BF),
            pltpu.SemaphoreType.DMA((16,)),
        ],
        compiler_params=params(56, 0),
        name="chip_sum",
    )(parts.reshape(PEERS, n, 128)).reshape(PACK, 128)


def place_kernel(core, half, *refs):
    conv, band, point, proj = refs[-4:]

    def place(out, n, start, cols):
        out[:, cols : cols + 128] = half[start : start + n, :].astype(F32)

    for t in range(TAPS):
        for n in range(2):
            place(conv.at[t], 128, (2 * t + n) * 128, 128 * n)
    for k in range(5):
        for n in range(4):
            place(band.at[k] if k < BANDS else point, 256, LATE + (4 * k + n) * 256, 128 * n)
    for n in range(2):
        place(proj, 256, LATE + (20 + n) * 256, 128 * n)


def place_half(core, half, before=()):
    any_ref = pl.BlockSpec(memory_space=pl.ANY)
    return pl.pallas_call(
        place_kernel,
        grid_spec=pltpu.PrefetchScalarGridSpec(
            num_scalar_prefetch=1,
            grid=(1,),
            in_specs=[pl.BlockSpec((PACK, 128), lambda i, c: (0, 0))] + [any_ref] * len(before),
            out_specs=[
                pl.BlockSpec((TAPS, 128, CF), lambda i, c: (0, c[0], 0)),
                pl.BlockSpec((BANDS, 256, C), lambda i, c: (0, c[0], 0)),
                pl.BlockSpec((256, C), lambda i, c: (c[0], 0)),
                pl.BlockSpec((256, CF), lambda i, c: (c[0], 0)),
            ],
        ),
        out_shape=[
            jax.ShapeDtypeStruct((TAPS, CF, CF), F32),
            jax.ShapeDtypeStruct((BANDS, C, C), F32),
            jax.ShapeDtypeStruct((C, C), F32),
            jax.ShapeDtypeStruct((C, CF), F32),
        ],
        input_output_aliases={2 + n: n for n in range(len(before))},
        compiler_params=params(16),
        cost_estimate=cost(0, 6_000_000),
        name="place_gradients",
    )(core, half, *before)


def shift(value, axes, count, step):
    pairs = [(i, i + step) for i in range(count) if 0 <= i + step < count]
    return lax.ppermute(value, axes, pairs)


def side_edges(first, last):
    lower = lax.axis_index("c") == 0
    twin = lax.ppermute(jnp.where(lower, last, first), "c", [(0, 1), (1, 0)])
    pairs = [(2 * k + 1, 2 * k + 2) for k in range(7)]
    pairs = pairs + [(b, a) for a, b in pairs]
    chip = lax.ppermute(jnp.where(lower, first, last), COL, pairs)
    return jnp.where(lower, chip, twin), jnp.where(lower, twin, chip)


def sides(corners, west, east):
    pad = jnp.zeros((SIDE - TR - 2, CF), BF)
    left = jnp.concatenate([corners[0], west, corners[2], pad], axis=0)
    right = jnp.concatenate([corners[1], east, corners[3], pad], axis=0)
    return left.astype(F32), right.astype(F32)


def row_halo(tile, west, east):
    low = jnp.concatenate([tile[TR - 1], west[TR - 1 :], east[TR - 1 :]], axis=0)
    high = jnp.concatenate([tile[0], west[:1], east[:1]], axis=0)
    even = lax.axis_index(ROW) % 2 == 0
    pairs = [(1, 2), (3, 4), (5, 6)]
    outer = lax.ppermute(jnp.where(even, high, low), ROW, pairs + [(b, a) for a, b in pairs])
    pairs = [(0, 1), (2, 3), (4, 5), (6, 7)]
    inner = lax.ppermute(jnp.where(even, low, high), ROW, pairs + [(b, a) for a, b in pairs])
    above, below = jnp.where(even, outer, inner), jnp.where(even, inner, outer)
    corners = [part for row in (above, below) for part in (row[TC : TC + 1], row[TC + 1 :])]
    return (jnp.stack([above[:TC], below[:TC]]),) + sides(corners, west, east)


def whole_halo(tile, first, last):
    lower = lax.axis_index("c") == 0
    inner, outer = jnp.where(lower, last, first), jnp.where(lower, first, last)
    twin = lax.ppermute(inner, "c", [(0, 1), (1, 0)])
    chips = [(2 * k + 1, 2 * k + 2) for k in range(7)]
    chips = chips + [(b, a) for a, b in chips]
    chip = lax.ppermute(outer, COL, chips)
    rows, far = [], []
    for down, at in ((1, TR - 1), (-1, 0)):
        rows.append(shift(jnp.concatenate([tile[at], twin[at : at + 1]], axis=0), ROW, 8, down))
        pairs = [(16 * r + a, 16 * (r + down) + b) for r in range(8) for a, b in chips if 0 <= r + down < 8]
        far.append(lax.ppermute(outer[at : at + 1], ROW + COL, pairs))
    west, east = jnp.where(lower, chip, twin), jnp.where(lower, twin, chip)
    corners = []
    for row, cell in zip(rows, far):
        near = row[TC:]
        corners += [jnp.where(lower, cell, near), jnp.where(lower, near, cell)]
    return (jnp.stack([row[:TC] for row in rows]),) + sides(corners, west, east)


def local(coarse_in, fine_in, band_weight, point_weight, proj_weight, conv_weight, out_cot):
    core = lax.axis_index("c").astype(jnp.int32).reshape(1)
    swap = [(0, 1), (1, 0)]

    chunks = coarse_in.reshape(2, 8, 16, C).transpose(1, 0, 2, 3)
    chunks = jnp.broadcast_to(chunks[:, None], (8, 2, 2, 16, C)).reshape(16, 2, 16, C)
    west, east = side_edges(out_cot[:, 0], out_cot[:, TC - 1])
    chunks, west, east = lax.optimization_barrier((chunks, west, east))
    cot_halo = row_halo(out_cot, west, east)
    x = lax.all_to_all(chunks, COL, 0, 0, tiled=True).reshape(PAIR, C)
    dco = dcoarse_pass(out_cot, *cot_halo, conv_weight)
    dtwin = lax.ppermute(dco, "c", swap)
    packed, conv_in, edges, keep, send = forward_pass(
        core, x, band_weight, point_weight, proj_weight, fine_in, out_cot, dco, dtwin, *cot_halo
    )
    got = lax.ppermute(send, "c", swap)
    late = (keep.astype(F32) + got.astype(F32)).astype(BF)
    packed = lax.dynamic_update_slice(packed, late, (0, 0))

    packed, conv_in, edges = lax.optimization_barrier((packed, conv_in, edges))
    parts = lax.all_to_all(packed, CHIPS, 0, 0, tiled=True)
    conv_halo = whole_halo(conv_in, edges[0], edges[1])
    spread = reduce_pass(parts)
    spread, conv_halo = lax.optimization_barrier((spread, conv_halo))
    mine = lax.all_to_all(spread, CHIPS, 0, 0, tiled=True)
    fine_out = conv_pass(conv_in, *conv_halo, conv_weight)
    mine, fine_out = lax.optimization_barrier((mine, fine_out))
    other = lax.ppermute(mine, "c", swap)
    grads = place_half(core, mine)
    grad_conv, grad_band, grad_point, grad_proj = place_half(1 - core, other, grads)
    return fine_out, grad_conv, grad_band, grad_point, grad_proj


def solution(mesh):
    fine_mesh = Mesh(
        np.asarray(mesh.devices).reshape([n for _, n in GRID]), tuple(name for name, _ in GRID)
    )
    fine = P(ROW, COL, None)
    in_specs = (P(ROW + COL, None, None), fine, P(), P(), P(), P(), fine)
    out_specs = (fine, P(), P(), P(), P())
    return jax.shard_map(local, mesh=fine_mesh, in_specs=in_specs, out_specs=out_specs, check_vma=False)
```

```python
import functools

import jax
import jax.numpy as jnp
import numpy as np
from jax import lax
from jax.experimental import pallas as pl
from jax.experimental.pallas import tpu as pltpu
from jax.sharding import Mesh
from jax.sharding import PartitionSpec as P

BF = jnp.bfloat16
F32 = jnp.float32
ROW = ("xl", "z")
COL = ("xh", "y", "c")
CHIPS = ("xl", "z", "xh", "y")
GRID = (("xl", 2), ("z", 4), ("xh", 2), ("y", 4), ("c", 2))

C, CF, BANDS, TAPS = 512, 256, 4, 9
TR, TC = 128, 32
IR, IC = 32, 8
CELLS = IR * IC
PAIR = 2 * CELLS
HB = 32
NB = TR // HB
SIDE = 136
LATE = TAPS * 2 * 128 + 256
EARLY = 5 * 4 * 256 + 2 * 256
PACK = LATE + EARLY
PEERS = 64
SCALE = float(1024 * 512) ** (-0.5)
MIB = 1024 * 1024
GELU_A = 0.7978845608028654
GELU_B = 0.044715


def params(mib, grid=1):
    return pltpu.CompilerParams(
        vmem_limit_bytes=mib * MIB, dimension_semantics=("arbitrary",) * grid if grid else None
    )


def cost(flops, moved):
    return pl.CostEstimate(flops=flops, bytes_accessed=moved, transcendentals=0)


def whole(*shape):
    return pl.BlockSpec(shape, lambda i: (0,) * len(shape))


def dot(a, b, dims=((1,), (0,))):
    return lax.dot_general(a, b, (dims, ((), ())), preferred_element_type=F32)


def iotas(*shape):
    return tuple(lax.broadcasted_iota(jnp.int32, shape, n) for n in range(len(shape)))


def haar_matrix():
    row, col = iotas(256, 256)
    inside = ((row >> 3) & 7 == col >> 5) & (row & 7 == (col & 15) >> 1)
    flip = ((row >> 6) & col & 1) ^ ((row >> 7) & (col >> 4) & 1)
    return jnp.where(inside, 0.5 - flip.astype(F32), 0.0).astype(BF)


def pool_matrix():
    row, col = iotas(TAPS * IC, 6 * TC)
    tap, j = row >> 3, row & 7
    a = (tap >= 3).astype(jnp.int32) + (tap >= 6).astype(jnp.int32)
    u = (col >> 5) + a - 2
    v = (col & 31) + (tap - 3 * a) - 1 - 4 * j
    return ((u >= 0) & (u < 4) & (v >= 0) & (v < 4)).astype(F32).astype(BF)


def side_matrix():
    row, col = iotas(3 * IR, SIDE)
    u = col + (row >> 5) - 2 - 4 * (row & 31)
    return ((u >= 0) & (u < 4)).astype(F32).astype(BF)


def dcoarse_kernel(oc, rows, left, right, wconv, out, pooled):
    pool, side = pool_matrix(), side_matrix()
    for i in range(IR):
        if i == 0:
            block = jnp.concatenate([rows[0], oc[: 5 * TC, :]], axis=0)
        elif i == IR - 1:
            block = jnp.concatenate([oc[(4 * i - 1) * TC :, :], rows[1]], axis=0)
        else:
            block = oc[(4 * i - 1) * TC : (4 * i + 5) * TC, :]
        part = dot(pool, block)
        for t in range(TAPS):
            for h in range(2):
                pooled[t, h, i * IC : (i + 1) * IC, :] = part[t * IC : (t + 1) * IC, h * 128 : (h + 1) * 128]
    for edge, b, start in ((left, 2, 0), (right, 0, IC - 1)):
        part = dot(side, edge[...].astype(BF))
        for a in range(3):
            for h in range(2):
                cells = pl.ds(start, IR, stride=IC)
                pooled[3 * a + b, h, cells, :] += part[a * IR : (a + 1) * IR, h * 128 : (h + 1) * 128]
    total = jnp.zeros((CELLS, CF), F32)
    for t in range(TAPS):
        s = jnp.concatenate([pooled[t, 0], pooled[t, 1]], axis=-1).astype(BF)
        total += dot(s, wconv[t], ((1,), (1,)))
    out[...] = total.astype(BF)


def dcoarse_pass(oc, rows, left, right, wconv):
    vm = pl.BlockSpec(memory_space=pltpu.VMEM)
    return pl.pallas_call(
        dcoarse_kernel,
        in_specs=[vm] * 5,
        out_specs=vm,
        out_shape=jax.ShapeDtypeStruct((CELLS, CF), BF),
        scratch_shapes=[pltpu.VMEM((TAPS, 2, CELLS, 128), F32)],
        compiler_params=params(16, 0),
        cost_estimate=cost(1_000, 1_000),
        name="coarse_cotangent",
    )(oc.reshape(TR * TC, CF), rows, left, right, wconv)


def coarse_gradients(core, haar, x, wproj, sub, slope, hidden, dco, dtwin, out, both):
    own = pl.multiple_of(core[0] * IC, IC)
    both[:, :, :, pl.ds(own, IC), :] = dco[...].astype(F32).reshape(8, 2, 2, IC, CF)
    both[:, :, :, pl.ds(IC - own, IC), :] = dtwin[...].astype(F32).reshape(8, 2, 2, IC, CF)
    d = jnp.concatenate([both[:, g].reshape(CELLS, CF) for g in range(2)], axis=0).astype(BF)
    dpre = (dot(d, wproj[...], ((1,), (1,))) * slope[...]).astype(BF)
    dmix = [dot(haar, dpre[g * 256 : (g + 1) * 256]).astype(BF) for g in range(2)]
    half = pl.ds(pl.multiple_of(core[0] * 256, 256), 256)
    for k in range(5):
        if k < BANDS:
            dk = jnp.concatenate([dmix[g][k * 64 : (k + 1) * 64] for g in range(2)], axis=0)
            grad = dot(sub[k * 128 : (k + 1) * 128, half], dk, ((0,), (0,)))
        else:
            grad = dot(x[:, half], dpre, ((0,), (0,)))
        for n in range(4):
            out[(4 * k + n) * 256 : (4 * k + n + 1) * 256, :] = grad[:, n * 128 : (n + 1) * 128].astype(BF)
    grad = dot(hidden[:, half], d, ((0,), (0,)))
    for n in range(2):
        out[(20 + n) * 256 : (21 + n) * 256, :] = grad[:, n * 128 : (n + 1) * 128].astype(BF)


def forward_kernel(
    core, x_hbm, xtwin_hbm, wb_hbm, wp_hbm, wj_hbm, fine_hbm, oc_hbm, dco, dtwin, rows, left, right,
    packed, conv_in, edges, keep, send,
    x, wband, wpoint, wproj, fine, oc, split, outs, up, ends, win, shifted, acc,
    sub, slope, hidden, early, both, sems,
):
    at = pl.multiple_of(core[0] * CELLS, CELLS)
    pairs = [(x_hbm, x.at[pl.ds(at, CELLS)])] + [(wb_hbm.at[k], wband.at[k]) for k in range(BANDS)]
    pairs += [(wp_hbm, wpoint), (wj_hbm, wproj), (fine_hbm, fine), (oc_hbm, oc)]
    pairs += [(xtwin_hbm, x.at[pl.ds(CELLS - at, CELLS)])]
    loads = [pltpu.make_async_copy(src, dst, sems.at[n]) for n, (src, dst) in enumerate(pairs)]
    store = pltpu.make_async_copy(early, packed.at[pl.ds(LATE, EARLY)], sems.at[len(pairs)])

    for load in loads[:1] + loads[-1:] + loads[1:-1]:
        load.start()
    haar = haar_matrix()
    loads[0].wait()
    loads[-1].wait()
    parts = [dot(haar, x[g * 256 : (g + 1) * 256, :]).astype(BF) for g in range(2)]
    for k in range(BANDS):
        part = jnp.concatenate([p[k * 64 : (k + 1) * 64] for p in parts], axis=0)
        sub[k * 128 : (k + 1) * 128, :] = part
        loads[1 + k].wait()
        m = dot(part, wband[k])
        hi = m.astype(BF)
        lo = (m - hi.astype(F32)).astype(BF)
        for g in range(2):
            split[g, 0, k * 64 : (k + 1) * 64, :] = hi[g * 64 : (g + 1) * 64]
            split[g, 1, k * 64 : (k + 1) * 64, :] = lo[g * 64 : (g + 1) * 64]
    loads[5].wait()
    loads[6].wait()
    for g in range(2):
        cells = slice(g * 256, (g + 1) * 256)
        value = dot(haar, split[g, 0], ((0,), (0,))) + dot(haar, split[g, 1], ((0,), (0,)))
        value = value + dot(x[cells, :], wpoint[...])
        square = value * value
        th = jnp.tanh(GELU_A * (value + GELU_B * (value * square)))
        slope[cells, :] = 0.5 * (1.0 + th) + 0.5 * value * (1.0 - th * th) * (GELU_A * (1.0 + 3.0 * GELU_B * square))
        act = (0.5 * value * (1.0 + th)).astype(BF)
        hidden[cells, :] = act
        outs[:, g] = dot(act, wproj[...]).astype(BF).astype(F32).reshape(8, 2, 16, CF)
    coarse_gradients(core, haar, x, wproj, sub, slope, hidden, dco, dtwin, early, both)
    store.start()
    loads[7].wait()
    loads[8].wait()

    def prepare(i):
        r0, slot = i * HB, i % 2
        for q in range(HB // 4):
            at = r0 // 4 + q
            cell = outs[at // 4, at // 2 % 2, at % 2, own, :]
            for s in range(4):
                up[slot, q, 0, pl.ds(s, IC, stride=4), :] = cell[:, :128]
                up[slot, q, 1, pl.ds(s, IC, stride=4), :] = cell[:, 128:]
            grown = jnp.concatenate([up[slot, q, 0], up[slot, q, 1]], axis=-1)
            for t in range(4):
                r = r0 + 4 * q + t
                value = fine[r].astype(F32) + grown
                fine[r] = value.astype(BF)
                ends[0, r : r + 1, :] = value[:1]
                ends[1, r : r + 1, :] = value[TC - 1 :]
        before = rows[0:1] if i == 0 else oc[r0 - 1 : r0]
        after = rows[1:2] if i == NB - 1 else oc[r0 + HB : r0 + HB + 1]
        fill_windows(r0, before, oc[r0 : r0 + HB], after, left, right, win.at[slot])
        for b in range(3):
            shifted[slot, :, :, b * CF : (b + 1) * CF] = win[slot, :, 9 - b : 9 - b + TC, :].astype(BF)

    def multiply(i):
        cells = fine[i * HB : (i + 1) * HB].reshape(HB * TC, CF).T
        for a in range(3):
            part = dot(cells, shifted[i % 2, 2 - a : 2 - a + HB].reshape(HB * TC, 3 * CF))
            acc[a] = part if i == 0 else acc[a] + part

    own = pl.ds(pl.multiple_of(core[0] * IC, IC), IC)
    prepare(0)
    for i in range(NB):
        if i + 1 < NB:
            prepare(i + 1)
        multiply(i)
    back = pltpu.make_async_copy(fine, conv_in, sems.at[len(pairs) + 1])
    back.start()
    edges[...] = ends[...].astype(BF)
    for out, c in ((keep, core[0]), (send, 1 - core[0])):
        half = pl.ds(pl.multiple_of(c * 128, 128), 128)
        for t in range(TAPS):
            for n in range(2):
                at = (t % 3) * CF + n * 128
                out[(2 * t + n) * 128 : (2 * t + n + 1) * 128, :] = acc[t // 3, half, at : at + 128].astype(BF)
        out[TAPS * 256 :, :] = jnp.zeros((LATE - TAPS * 256, 128), BF)
    store.wait()
    back.wait()


def forward_pass(core, x, xtwin, wband, wpoint, wproj, fine, oc, dco, dtwin, rows, left, right):
    hbm, vm = pl.BlockSpec(memory_space=pltpu.HBM), pl.BlockSpec(memory_space=pltpu.VMEM)
    return pl.pallas_call(
        forward_kernel,
        in_specs=[pl.BlockSpec(memory_space=pltpu.SMEM)]
        + [hbm] * 7
        + [vm] * 5,
        out_specs=[hbm, hbm, vm, vm, vm],
        out_shape=[
            jax.ShapeDtypeStruct((PACK, 128), BF),
            jax.ShapeDtypeStruct((TR, TC, CF), BF),
            jax.ShapeDtypeStruct((2, TR, CF), BF),
            jax.ShapeDtypeStruct((LATE, 128), BF),
            jax.ShapeDtypeStruct((LATE, 128), BF),
        ],
        scratch_shapes=[
            pltpu.VMEM((PAIR, C), BF),
            pltpu.VMEM((BANDS, C, C), BF),
            pltpu.VMEM((C, C), BF),
            pltpu.VMEM((C, CF), BF),
            pltpu.VMEM((TR, TC, CF), BF),
            pltpu.VMEM((TR, TC, CF), BF),
            pltpu.VMEM((2, 2, 256, C), BF),
            pltpu.VMEM((8, 2, 2, 2 * IC, CF), F32),
            pltpu.VMEM((2, HB // 4, 2, TC, 128), F32),
            pltpu.VMEM((2, TR, CF), F32),
            pltpu.VMEM((2, HB + 2, 48, CF), F32),
            pltpu.VMEM((2, HB + 2, TC, 3 * CF), BF),
            pltpu.VMEM((3, CF, 3 * CF), F32),
            pltpu.VMEM((PAIR, C), BF),
            pltpu.VMEM((PAIR, C), F32),
            pltpu.VMEM((PAIR, C), BF),
            pltpu.VMEM((EARLY, 128), BF),
            pltpu.VMEM((8, 2, 2, 2 * IC, CF), F32),
            pltpu.SemaphoreType.DMA((12,)),
        ],
        compiler_params=params(56, 0),
        cost_estimate=cost(8_000_000_000, 14_000_000),
        name="forward_and_gradients",
    )(core, x, xtwin, wband, wpoint, wproj, fine, oc, dco, dtwin, rows, left, right)


def window_specs():
    return [
        pl.BlockSpec((1, TC, CF), lambda i: (jnp.maximum(i * HB - 1, 0), 0, 0)),
        pl.BlockSpec((HB, TC, CF), lambda i: (i, 0, 0)),
        pl.BlockSpec((1, TC, CF), lambda i: (jnp.minimum(i * HB + HB, TR - 1), 0, 0)),
        whole(2, TC, CF),
        whole(SIDE, CF),
        whole(SIDE, CF),
    ]


def fill_windows(r0, before, tile, after, left, right, win):
    win[1 : HB + 1, 8 : 8 + TC, :] = tile.astype(F32)
    win[0:1, 8 : 8 + TC, :] = before.astype(F32)
    win[HB + 1 : HB + 2, 8 : 8 + TC, :] = after.astype(F32)
    for r in range(HB + 2):
        win[r, 7:8, :] = left[pl.ds(r0 + r, 1), :]
        win[r, 8 + TC : 9 + TC, :] = right[pl.ds(r0 + r, 1), :]


def conv_kernel(before, ci, after, rows, left, right, wconv, out, win, wide):
    i = pl.program_id(0)
    above = jnp.where(i == 0, rows[0:1], before[...])
    below = jnp.where(i == NB - 1, rows[1:2], after[...])
    fill_windows(i * HB, above, ci[...], below, left, right, win)
    for b in range(3):
        wide[:, :, b * CF : (b + 1) * CF] = win[:, 7 + b : 7 + b + TC, :].astype(BF)
    total = jnp.zeros((HB * TC, CF), F32)
    for a in range(3):
        total += dot(wide[a : a + HB].reshape(HB * TC, 3 * CF), wconv[a])
    out[...] = total.astype(BF).reshape(HB, TC, CF)


def conv_pass(ci, rows, left, right, wconv):
    return pl.pallas_call(
        conv_kernel,
        grid=(NB,),
        in_specs=window_specs() + [whole(3, 3 * CF, CF)],
        out_specs=pl.BlockSpec((HB, TC, CF), lambda i: (i, 0, 0)),
        out_shape=jax.ShapeDtypeStruct((TR, TC, CF), BF),
        scratch_shapes=[pltpu.VMEM((HB + 2, 48, CF), F32), pltpu.VMEM((HB + 2, TC, 3 * CF), BF)],
        compiler_params=params(16),
        cost_estimate=cost(1_000_000, 1_000_000),
        name="conv_forward",
    )(ci, ci, ci, rows, left, right, wconv.reshape(3, 3 * CF, CF))


def reduce_kernel(parts, out, held, copies, sems):
    n = PEERS // 8
    loads = [pltpu.make_async_copy(parts.at[pl.ds(g * n, n)], held.at[g], sems.at[g]) for g in range(8)]
    for load in loads:
        load.start()
    total = None
    for g in range(8):
        loads[g].wait()
        part = jnp.sum(held[g].astype(F32), axis=0)
        total = part if total is None else total + part
    done = (total * SCALE).astype(BF)
    for p in range(n):
        copies[p] = done
    stores = [pltpu.make_async_copy(copies, out.at[pl.ds(g * n, n)], sems.at[8 + g]) for g in range(8)]
    for store in stores:
        store.start()
    for store in stores:
        store.wait()


def reduce_pass(parts):
    n = PACK // PEERS
    hbm = pl.BlockSpec(memory_space=pltpu.HBM)
    return pl.pallas_call(
        reduce_kernel,
        in_specs=[hbm],
        out_specs=hbm,
        out_shape=jax.ShapeDtypeStruct((PEERS, n, 128), BF),
        scratch_shapes=[
            pltpu.VMEM((8, PEERS // 8, n, 128), BF),
            pltpu.VMEM((PEERS // 8, n, 128), BF),
            pltpu.SemaphoreType.DMA((16,)),
        ],
        compiler_params=params(56, 0),
        name="chip_sum",
    )(parts.reshape(PEERS, n, 128)).reshape(PACK, 128)


def place_kernel(core, half, *refs):
    conv, band, point, proj = refs[-4:]

    def place(out, n, start, cols):
        out[:, cols : cols + 128] = half[start : start + n, :].astype(F32)

    for t in range(TAPS):
        for n in range(2):
            place(conv.at[t], 128, (2 * t + n) * 128, 128 * n)
    for k in range(5):
        for n in range(4):
            place(band.at[k] if k < BANDS else point, 256, LATE + (4 * k + n) * 256, 128 * n)
    for n in range(2):
        place(proj, 256, LATE + (20 + n) * 256, 128 * n)


def place_half(core, half, before=()):
    any_ref = pl.BlockSpec(memory_space=pl.ANY)
    return pl.pallas_call(
        place_kernel,
        grid_spec=pltpu.PrefetchScalarGridSpec(
            num_scalar_prefetch=1,
            grid=(1,),
            in_specs=[pl.BlockSpec((PACK, 128), lambda i, c: (0, 0))] + [any_ref] * len(before),
            out_specs=[
                pl.BlockSpec((TAPS, 128, CF), lambda i, c: (0, c[0], 0)),
                pl.BlockSpec((BANDS, 256, C), lambda i, c: (0, c[0], 0)),
                pl.BlockSpec((256, C), lambda i, c: (c[0], 0)),
                pl.BlockSpec((256, CF), lambda i, c: (c[0], 0)),
            ],
        ),
        out_shape=[
            jax.ShapeDtypeStruct((TAPS, CF, CF), F32),
            jax.ShapeDtypeStruct((BANDS, C, C), F32),
            jax.ShapeDtypeStruct((C, C), F32),
            jax.ShapeDtypeStruct((C, CF), F32),
        ],
        input_output_aliases={2 + n: n for n in range(len(before))},
        compiler_params=params(16),
        cost_estimate=cost(0, 6_000_000),
        name="place_gradients",
    )(core, half, *before)


def shift(value, axes, count, step):
    pairs = [(i, i + step) for i in range(count) if 0 <= i + step < count]
    return lax.ppermute(value, axes, pairs)


def side_edges(first, last):
    lower = lax.axis_index("c") == 0
    twin = lax.ppermute(jnp.where(lower, last, first), "c", [(0, 1), (1, 0)])
    pairs = [(2 * k + 1, 2 * k + 2) for k in range(7)]
    pairs = pairs + [(b, a) for a, b in pairs]
    chip = lax.ppermute(jnp.where(lower, first, last), COL, pairs)
    return jnp.where(lower, chip, twin), jnp.where(lower, twin, chip)


def sides(corners, west, east):
    pad = jnp.zeros((SIDE - TR - 2, CF), BF)
    left = jnp.concatenate([corners[0], west, corners[2], pad], axis=0)
    right = jnp.concatenate([corners[1], east, corners[3], pad], axis=0)
    return left.astype(F32), right.astype(F32)


def row_halo(tile, west, east):
    low = jnp.concatenate([tile[TR - 1], west[TR - 1 :], east[TR - 1 :]], axis=0)
    high = jnp.concatenate([tile[0], west[:1], east[:1]], axis=0)
    even = lax.axis_index(ROW) % 2 == 0
    pairs = [(1, 2), (3, 4), (5, 6)]
    outer = lax.ppermute(jnp.where(even, high, low), ROW, pairs + [(b, a) for a, b in pairs])
    pairs = [(0, 1), (2, 3), (4, 5), (6, 7)]
    inner = lax.ppermute(jnp.where(even, low, high), ROW, pairs + [(b, a) for a, b in pairs])
    above, below = jnp.where(even, outer, inner), jnp.where(even, inner, outer)
    corners = [part for row in (above, below) for part in (row[TC : TC + 1], row[TC + 1 :])]
    return (jnp.stack([above[:TC], below[:TC]]),) + sides(corners, west, east)


def whole_halo(tile, first, last):
    lower = lax.axis_index("c") == 0
    inner, outer = jnp.where(lower, last, first), jnp.where(lower, first, last)
    twin = lax.ppermute(inner, "c", [(0, 1), (1, 0)])
    chips = [(2 * k + 1, 2 * k + 2) for k in range(7)]
    chips = chips + [(b, a) for a, b in chips]
    chip = lax.ppermute(outer, COL, chips)
    rows, far = [], []
    for down, at in ((1, TR - 1), (-1, 0)):
        rows.append(shift(jnp.concatenate([tile[at], twin[at : at + 1]], axis=0), ROW, 8, down))
        pairs = [(16 * r + a, 16 * (r + down) + b) for r in range(8) for a, b in chips if 0 <= r + down < 8]
        far.append(lax.ppermute(outer[at : at + 1], ROW + COL, pairs))
    west, east = jnp.where(lower, chip, twin), jnp.where(lower, twin, chip)
    corners = []
    for row, cell in zip(rows, far):
        near = row[TC:]
        corners += [jnp.where(lower, cell, near), jnp.where(lower, near, cell)]
    return (jnp.stack([row[:TC] for row in rows]),) + sides(corners, west, east)


def local(coarse_in, fine_in, band_weight, point_weight, proj_weight, conv_weight, out_cot):
    core = lax.axis_index("c").astype(jnp.int32).reshape(1)
    swap = [(0, 1), (1, 0)]

    chunks = coarse_in.reshape(2, 8, 16, C).transpose(1, 0, 2, 3)
    west, east = side_edges(out_cot[:, 0], out_cot[:, TC - 1])
    chunks, west, east = lax.optimization_barrier((chunks, west, east))
    cot_halo = row_halo(out_cot, west, east)
    x = lax.all_to_all(chunks, ("xh", "y"), 0, 0, tiled=True).reshape(CELLS, C)
    dco = dcoarse_pass(out_cot, *cot_halo, conv_weight)
    x, dco = lax.optimization_barrier((x, dco))
    xtwin, dtwin = lax.ppermute(x, "c", swap), lax.ppermute(dco, "c", swap)
    packed, conv_in, edges, keep, send = forward_pass(
        core, x, xtwin, band_weight, point_weight, proj_weight, fine_in, out_cot, dco, dtwin, *cot_halo
    )
    got = lax.ppermute(send, "c", swap)
    late = (keep.astype(F32) + got.astype(F32)).astype(BF)
    packed = lax.dynamic_update_slice(packed, late, (0, 0))

    packed, conv_in, edges = lax.optimization_barrier((packed, conv_in, edges))
    parts = lax.all_to_all(packed, CHIPS, 0, 0, tiled=True)
    conv_halo = whole_halo(conv_in, edges[0], edges[1])
    spread = reduce_pass(parts)
    spread, conv_halo = lax.optimization_barrier((spread, conv_halo))
    mine = lax.all_to_all(spread, CHIPS, 0, 0, tiled=True)
    fine_out = conv_pass(conv_in, *conv_halo, conv_weight)
    mine, fine_out = lax.optimization_barrier((mine, fine_out))
    other = lax.ppermute(mine, "c", swap)
    grads = place_half(core, mine)
    grad_conv, grad_band, grad_point, grad_proj = place_half(1 - core, other, grads)
    return fine_out, grad_conv, grad_band, grad_point, grad_proj


def solution(mesh):
    fine_mesh = Mesh(
        np.asarray(mesh.devices).reshape([n for _, n in GRID]), tuple(name for name, _ in GRID)
    )
    fine = P(ROW, COL, None)
    in_specs = (P(ROW + COL, None, None), fine, P(), P(), P(), P(), fine)
    out_specs = (fine, P(), P(), P(), P())
    return jax.shard_map(local, mesh=fine_mesh, in_specs=in_specs, out_specs=out_specs, check_vma=False)
```

```python
import functools

import jax
import jax.numpy as jnp
import numpy as np
from jax import lax
from jax.experimental import pallas as pl
from jax.experimental.pallas import tpu as pltpu
from jax.sharding import Mesh
from jax.sharding import PartitionSpec as P

BF = jnp.bfloat16
F32 = jnp.float32
ROW = ("xl", "z")
COL = ("xh", "y", "c")
CHIPS = ("xl", "z", "xh", "y")
GRID = (("xl", 2), ("z", 4), ("xh", 2), ("y", 4), ("c", 2))

C, CF, BANDS, TAPS = 512, 256, 4, 9
TR, TC = 128, 32
IR, IC = 32, 8
CELLS = IR * IC
PAIR = 2 * CELLS
HB = 32
NB = TR // HB
SIDE = 136
LATE = TAPS * 2 * 128 + 256
EARLY = 5 * 4 * 256 + 2 * 256
PACK = LATE + EARLY
PEERS = 64
SCALE = float(1024 * 512) ** (-0.5)
MIB = 1024 * 1024
GELU_A = 0.7978845608028654
GELU_B = 0.044715


def params(mib, grid=1):
    return pltpu.CompilerParams(
        vmem_limit_bytes=mib * MIB, dimension_semantics=("arbitrary",) * grid if grid else None
    )


def cost(flops, moved):
    return pl.CostEstimate(flops=flops, bytes_accessed=moved, transcendentals=0)


def whole(*shape):
    return pl.BlockSpec(shape, lambda i: (0,) * len(shape))


def dot(a, b, dims=((1,), (0,))):
    return lax.dot_general(a, b, (dims, ((), ())), preferred_element_type=F32)


def iotas(*shape):
    return tuple(lax.broadcasted_iota(jnp.int32, shape, n) for n in range(len(shape)))


def haar_matrix():
    row, col = iotas(256, 256)
    inside = ((row >> 3) & 7 == col >> 5) & (row & 7 == (col & 15) >> 1)
    flip = ((row >> 6) & col & 1) ^ ((row >> 7) & (col >> 4) & 1)
    return jnp.where(inside, 0.5 - flip.astype(F32), 0.0).astype(BF)


def pool_matrix():
    row, col = iotas(TAPS * IC, 6 * TC)
    tap, j = row >> 3, row & 7
    a = (tap >= 3).astype(jnp.int32) + (tap >= 6).astype(jnp.int32)
    u = (col >> 5) + a - 2
    v = (col & 31) + (tap - 3 * a) - 1 - 4 * j
    return ((u >= 0) & (u < 4) & (v >= 0) & (v < 4)).astype(F32).astype(BF)


def side_matrix():
    row, col = iotas(3 * IR, SIDE)
    u = col + (row >> 5) - 2 - 4 * (row & 31)
    return ((u >= 0) & (u < 4)).astype(F32).astype(BF)


def dcoarse_kernel(oc, rows, left, right, wconv, out, pooled):
    pool, side = pool_matrix(), side_matrix()
    for i in range(IR):
        if i == 0:
            block = jnp.concatenate([rows[0], oc[: 5 * TC, :]], axis=0)
        elif i == IR - 1:
            block = jnp.concatenate([oc[(4 * i - 1) * TC :, :], rows[1]], axis=0)
        else:
            block = oc[(4 * i - 1) * TC : (4 * i + 5) * TC, :]
        part = dot(pool, block)
        for t in range(TAPS):
            for h in range(2):
                pooled[t, h, i * IC : (i + 1) * IC, :] = part[t * IC : (t + 1) * IC, h * 128 : (h + 1) * 128]
    for edge, b, start in ((left, 2, 0), (right, 0, IC - 1)):
        part = dot(side, edge[...].astype(BF))
        for a in range(3):
            for h in range(2):
                cells = pl.ds(start, IR, stride=IC)
                pooled[3 * a + b, h, cells, :] += part[a * IR : (a + 1) * IR, h * 128 : (h + 1) * 128]
    total = jnp.zeros((CELLS, CF), F32)
    for t in range(TAPS):
        s = jnp.concatenate([pooled[t, 0], pooled[t, 1]], axis=-1).astype(BF)
        total += dot(s, wconv[t], ((1,), (1,)))
    out[...] = total.astype(BF)


def dcoarse_pass(oc, rows, left, right, wconv):
    vm = pl.BlockSpec(memory_space=pltpu.VMEM)
    return pl.pallas_call(
        dcoarse_kernel,
        in_specs=[vm] * 5,
        out_specs=vm,
        out_shape=jax.ShapeDtypeStruct((CELLS, CF), BF),
        scratch_shapes=[pltpu.VMEM((TAPS, 2, CELLS, 128), F32)],
        compiler_params=params(16, 0),
        cost_estimate=cost(1_000, 1_000),
        name="coarse_cotangent",
    )(oc.reshape(TR * TC, CF), rows, left, right, wconv)


def coarse_gradients(core, haar, x, wproj, sub, slope, hidden, dco, dtwin, out, both):
    own = pl.multiple_of(core[0] * IC, IC)
    both[:, :, :, pl.ds(own, IC), :] = dco[...].astype(F32).reshape(8, 2, 2, IC, CF)
    both[:, :, :, pl.ds(IC - own, IC), :] = dtwin[...].astype(F32).reshape(8, 2, 2, IC, CF)
    d = jnp.concatenate([both[:, g].reshape(CELLS, CF) for g in range(2)], axis=0).astype(BF)
    dpre = (dot(d, wproj[...], ((1,), (1,))) * slope[...]).astype(BF)
    dmix = [dot(haar, dpre[g * 256 : (g + 1) * 256]).astype(BF) for g in range(2)]
    half = pl.ds(pl.multiple_of(core[0] * 256, 256), 256)
    for k in range(5):
        if k < BANDS:
            dk = jnp.concatenate([dmix[g][k * 64 : (k + 1) * 64] for g in range(2)], axis=0)
            grad = dot(sub[k * 128 : (k + 1) * 128, half], dk, ((0,), (0,)))
        else:
            grad = dot(x[:, half], dpre, ((0,), (0,)))
        for n in range(4):
            out[(4 * k + n) * 256 : (4 * k + n + 1) * 256, :] = grad[:, n * 128 : (n + 1) * 128].astype(BF)
    grad = dot(hidden[:, half], d, ((0,), (0,)))
    for n in range(2):
        out[(20 + n) * 256 : (21 + n) * 256, :] = grad[:, n * 128 : (n + 1) * 128].astype(BF)


def forward_kernel(
    core, x_hbm, xtwin_hbm, wb_hbm, wp_hbm, wj_hbm, fine_hbm, oc_hbm, dco, dtwin, rows, left, right,
    packed, conv_in, edges, keep, send,
    x, wband, wpoint, wproj, fine, oc, split, outs, up, ends, win, shifted, acc,
    sub, slope, hidden, early, both, sems,
):
    at = pl.multiple_of(core[0] * CELLS, CELLS)
    pairs = [(x_hbm, x.at[pl.ds(at, CELLS)])] + [(wb_hbm.at[k], wband.at[k]) for k in range(BANDS)]
    pairs += [(wp_hbm, wpoint), (wj_hbm, wproj), (fine_hbm, fine), (oc_hbm, oc)]
    pairs += [(xtwin_hbm, x.at[pl.ds(CELLS - at, CELLS)])]
    loads = [pltpu.make_async_copy(src, dst, sems.at[n]) for n, (src, dst) in enumerate(pairs)]
    store = pltpu.make_async_copy(early, packed.at[pl.ds(LATE, EARLY)], sems.at[len(pairs)])

    for load in loads[:1] + loads[-1:] + loads[1:-1]:
        load.start()
    haar = haar_matrix()
    loads[0].wait()
    loads[-1].wait()
    parts = [dot(haar, x[g * 256 : (g + 1) * 256, :]).astype(BF) for g in range(2)]
    for k in range(BANDS):
        part = jnp.concatenate([p[k * 64 : (k + 1) * 64] for p in parts], axis=0)
        sub[k * 128 : (k + 1) * 128, :] = part
        loads[1 + k].wait()
        m = dot(part, wband[k])
        hi = m.astype(BF)
        lo = (m - hi.astype(F32)).astype(BF)
        for g in range(2):
            split[g, 0, k * 64 : (k + 1) * 64, :] = hi[g * 64 : (g + 1) * 64]
            split[g, 1, k * 64 : (k + 1) * 64, :] = lo[g * 64 : (g + 1) * 64]
    loads[5].wait()
    loads[6].wait()
    for g in range(2):
        cells = slice(g * 256, (g + 1) * 256)
        value = dot(haar, split[g, 0], ((0,), (0,))) + dot(haar, split[g, 1], ((0,), (0,)))
        value = value + dot(x[cells, :], wpoint[...])
        square = value * value
        th = jnp.tanh(GELU_A * (value + GELU_B * (value * square)))
        slope[cells, :] = 0.5 * (1.0 + th) + 0.5 * value * (1.0 - th * th) * (GELU_A * (1.0 + 3.0 * GELU_B * square))
        act = (0.5 * value * (1.0 + th)).astype(BF)
        hidden[cells, :] = act
        outs[:, g] = dot(act, wproj[...]).astype(BF).astype(F32).reshape(8, 2, 16, CF)
    coarse_gradients(core, haar, x, wproj, sub, slope, hidden, dco, dtwin, early, both)
    store.start()
    loads[7].wait()
    loads[8].wait()

    def prepare(i):
        r0, slot = i * HB, i % 2
        for q in range(HB // 4):
            at = r0 // 4 + q
            cell = outs[at // 4, at // 2 % 2, at % 2, own, :]
            for s in range(4):
                up[slot, q, 0, pl.ds(s, IC, stride=4), :] = cell[:, :128]
                up[slot, q, 1, pl.ds(s, IC, stride=4), :] = cell[:, 128:]
            grown = jnp.concatenate([up[slot, q, 0], up[slot, q, 1]], axis=-1)
            for t in range(4):
                r = r0 + 4 * q + t
                value = fine[r].astype(F32) + grown
                fine[r] = value.astype(BF)
                ends[0, r : r + 1, :] = value[:1]
                ends[1, r : r + 1, :] = value[TC - 1 :]
        before = rows[0:1] if i == 0 else oc[r0 - 1 : r0]
        after = rows[1:2] if i == NB - 1 else oc[r0 + HB : r0 + HB + 1]
        fill_windows(r0, before, oc[r0 : r0 + HB], after, left, right, win.at[slot])
        for b in range(3):
            shifted[slot, :, :, b * CF : (b + 1) * CF] = win[slot, :, 9 - b : 9 - b + TC, :].astype(BF)

    def multiply(i):
        cells = fine[i * HB : (i + 1) * HB].reshape(HB * TC, CF).T
        for a in range(3):
            part = dot(cells, shifted[i % 2, 2 - a : 2 - a + HB].reshape(HB * TC, 3 * CF))
            acc[a] = part if i == 0 else acc[a] + part

    own = pl.ds(pl.multiple_of(core[0] * IC, IC), IC)
    prepare(0)
    for i in range(NB):
        if i + 1 < NB:
            prepare(i + 1)
        multiply(i)
    back = pltpu.make_async_copy(fine, conv_in, sems.at[len(pairs) + 1])
    back.start()
    edges[...] = ends[...].astype(BF)
    for out, c in ((keep, core[0]), (send, 1 - core[0])):
        half = pl.ds(pl.multiple_of(c * 128, 128), 128)
        for t in range(TAPS):
            for n in range(2):
                at = (t % 3) * CF + n * 128
                out[(2 * t + n) * 128 : (2 * t + n + 1) * 128, :] = acc[t // 3, half, at : at + 128].astype(BF)
        out[TAPS * 256 :, :] = jnp.zeros((LATE - TAPS * 256, 128), BF)
    store.wait()
    back.wait()


def forward_pass(core, x, xtwin, wband, wpoint, wproj, fine, oc, dco, dtwin, rows, left, right):
    hbm, vm = pl.BlockSpec(memory_space=pltpu.HBM), pl.BlockSpec(memory_space=pltpu.VMEM)
    return pl.pallas_call(
        forward_kernel,
        in_specs=[pl.BlockSpec(memory_space=pltpu.SMEM)]
        + [hbm] * 7
        + [vm] * 5,
        out_specs=[hbm, hbm, vm, vm, vm],
        out_shape=[
            jax.ShapeDtypeStruct((PACK, 128), BF),
            jax.ShapeDtypeStruct((TR, TC, CF), BF),
            jax.ShapeDtypeStruct((2, TR, CF), BF),
            jax.ShapeDtypeStruct((LATE, 128), BF),
            jax.ShapeDtypeStruct((LATE, 128), BF),
        ],
        scratch_shapes=[
            pltpu.VMEM((PAIR, C), BF),
            pltpu.VMEM((BANDS, C, C), BF),
            pltpu.VMEM((C, C), BF),
            pltpu.VMEM((C, CF), BF),
            pltpu.VMEM((TR, TC, CF), BF),
            pltpu.VMEM((TR, TC, CF), BF),
            pltpu.VMEM((2, 2, 256, C), BF),
            pltpu.VMEM((8, 2, 2, 2 * IC, CF), F32),
            pltpu.VMEM((2, HB // 4, 2, TC, 128), F32),
            pltpu.VMEM((2, TR, CF), F32),
            pltpu.VMEM((2, HB + 2, 48, CF), F32),
            pltpu.VMEM((2, HB + 2, TC, 3 * CF), BF),
            pltpu.VMEM((3, CF, 3 * CF), F32),
            pltpu.VMEM((PAIR, C), BF),
            pltpu.VMEM((PAIR, C), F32),
            pltpu.VMEM((PAIR, C), BF),
            pltpu.VMEM((EARLY, 128), BF),
            pltpu.VMEM((8, 2, 2, 2 * IC, CF), F32),
            pltpu.SemaphoreType.DMA((12,)),
        ],
        compiler_params=params(50, 0),
        cost_estimate=cost(8_000_000_000, 14_000_000),
        name="forward_and_gradients",
    )(core, x, xtwin, wband, wpoint, wproj, fine, oc, dco, dtwin, rows, left, right)


def window_specs():
    return [
        pl.BlockSpec((1, TC, CF), lambda i: (jnp.maximum(i * HB - 1, 0), 0, 0)),
        pl.BlockSpec((HB, TC, CF), lambda i: (i, 0, 0)),
        pl.BlockSpec((1, TC, CF), lambda i: (jnp.minimum(i * HB + HB, TR - 1), 0, 0)),
        whole(2, TC, CF),
        whole(SIDE, CF),
        whole(SIDE, CF),
    ]


def fill_windows(r0, before, tile, after, left, right, win):
    win[1 : HB + 1, 8 : 8 + TC, :] = tile.astype(F32)
    win[0:1, 8 : 8 + TC, :] = before.astype(F32)
    win[HB + 1 : HB + 2, 8 : 8 + TC, :] = after.astype(F32)
    for r in range(HB + 2):
        win[r, 7:8, :] = left[pl.ds(r0 + r, 1), :]
        win[r, 8 + TC : 9 + TC, :] = right[pl.ds(r0 + r, 1), :]


def conv_kernel(before, ci, after, rows, left, right, wconv, out, win, wide):
    i = pl.program_id(0)
    above = jnp.where(i == 0, rows[0:1], before[...])
    below = jnp.where(i == NB - 1, rows[1:2], after[...])
    fill_windows(i * HB, above, ci[...], below, left, right, win)
    for b in range(3):
        wide[:, :, b * CF : (b + 1) * CF] = win[:, 7 + b : 7 + b + TC, :].astype(BF)
    total = jnp.zeros((HB * TC, CF), F32)
    for a in range(3):
        total += dot(wide[a : a + HB].reshape(HB * TC, 3 * CF), wconv[a])
    out[...] = total.astype(BF).reshape(HB, TC, CF)


def conv_pass(ci, rows, left, right, wconv):
    return pl.pallas_call(
        conv_kernel,
        grid=(NB,),
        in_specs=window_specs() + [whole(3, 3 * CF, CF)],
        out_specs=pl.BlockSpec((HB, TC, CF), lambda i: (i, 0, 0)),
        out_shape=jax.ShapeDtypeStruct((TR, TC, CF), BF),
        scratch_shapes=[pltpu.VMEM((HB + 2, 48, CF), F32), pltpu.VMEM((HB + 2, TC, 3 * CF), BF)],
        compiler_params=params(16),
        cost_estimate=cost(1_000_000, 1_000_000),
        name="conv_forward",
    )(ci, ci, ci, rows, left, right, wconv.reshape(3, 3 * CF, CF))


def reduce_kernel(parts, out, held, copies, sems):
    n = PEERS // 8
    loads = [pltpu.make_async_copy(parts.at[pl.ds(g * n, n)], held.at[g], sems.at[g]) for g in range(8)]
    for load in loads:
        load.start()
    total = None
    for g in range(8):
        loads[g].wait()
        part = jnp.sum(held[g].astype(F32), axis=0)
        total = part if total is None else total + part
    done = (total * SCALE).astype(BF)
    for p in range(n):
        copies[p] = done
    stores = [pltpu.make_async_copy(copies, out.at[pl.ds(g * n, n)], sems.at[8 + g]) for g in range(8)]
    for store in stores:
        store.start()
    for store in stores:
        store.wait()


def reduce_pass(parts):
    n = PACK // PEERS
    hbm = pl.BlockSpec(memory_space=pltpu.HBM)
    return pl.pallas_call(
        reduce_kernel,
        in_specs=[hbm],
        out_specs=hbm,
        out_shape=jax.ShapeDtypeStruct((PEERS, n, 128), BF),
        scratch_shapes=[
            pltpu.VMEM((8, PEERS // 8, n, 128), BF),
            pltpu.VMEM((PEERS // 8, n, 128), BF),
            pltpu.SemaphoreType.DMA((16,)),
        ],
        compiler_params=params(56, 0),
        name="chip_sum",
    )(parts.reshape(PEERS, n, 128)).reshape(PACK, 128)


def place_kernel(core, half, *refs):
    conv, band, point, proj = refs[-4:]

    def place(out, n, start, cols):
        out[:, cols : cols + 128] = half[start : start + n, :].astype(F32)

    for t in range(TAPS):
        for n in range(2):
            place(conv.at[t], 128, (2 * t + n) * 128, 128 * n)
    for k in range(5):
        for n in range(4):
            place(band.at[k] if k < BANDS else point, 256, LATE + (4 * k + n) * 256, 128 * n)
    for n in range(2):
        place(proj, 256, LATE + (20 + n) * 256, 128 * n)


def place_half(core, half, before=()):
    any_ref = pl.BlockSpec(memory_space=pl.ANY)
    return pl.pallas_call(
        place_kernel,
        grid_spec=pltpu.PrefetchScalarGridSpec(
            num_scalar_prefetch=1,
            grid=(1,),
            in_specs=[pl.BlockSpec((PACK, 128), lambda i, c: (0, 0))] + [any_ref] * len(before),
            out_specs=[
                pl.BlockSpec((TAPS, 128, CF), lambda i, c: (0, c[0], 0)),
                pl.BlockSpec((BANDS, 256, C), lambda i, c: (0, c[0], 0)),
                pl.BlockSpec((256, C), lambda i, c: (c[0], 0)),
                pl.BlockSpec((256, CF), lambda i, c: (c[0], 0)),
            ],
        ),
        out_shape=[
            jax.ShapeDtypeStruct((TAPS, CF, CF), F32),
            jax.ShapeDtypeStruct((BANDS, C, C), F32),
            jax.ShapeDtypeStruct((C, C), F32),
            jax.ShapeDtypeStruct((C, CF), F32),
        ],
        input_output_aliases={2 + n: n for n in range(len(before))},
        compiler_params=params(16),
        cost_estimate=cost(0, 6_000_000),
        name="place_gradients",
    )(core, half, *before)


def shift(value, axes, count, step):
    pairs = [(i, i + step) for i in range(count) if 0 <= i + step < count]
    return lax.ppermute(value, axes, pairs)


def side_edges(first, last):
    lower = lax.axis_index("c") == 0
    twin = lax.ppermute(jnp.where(lower, last, first), "c", [(0, 1), (1, 0)])
    pairs = [(2 * k + 1, 2 * k + 2) for k in range(7)]
    pairs = pairs + [(b, a) for a, b in pairs]
    chip = lax.ppermute(jnp.where(lower, first, last), COL, pairs)
    return jnp.where(lower, chip, twin), jnp.where(lower, twin, chip)


def sides(corners, west, east):
    pad = jnp.zeros((SIDE - TR - 2, CF), BF)
    left = jnp.concatenate([corners[0], west, corners[2], pad], axis=0)
    right = jnp.concatenate([corners[1], east, corners[3], pad], axis=0)
    return left.astype(F32), right.astype(F32)


def row_halo(tile, west, east):
    low = jnp.concatenate([tile[TR - 1], west[TR - 1 :], east[TR - 1 :]], axis=0)
    high = jnp.concatenate([tile[0], west[:1], east[:1]], axis=0)
    even = lax.axis_index(ROW) % 2 == 0
    pairs = [(1, 2), (3, 4), (5, 6)]
    outer = lax.ppermute(jnp.where(even, high, low), ROW, pairs + [(b, a) for a, b in pairs])
    pairs = [(0, 1), (2, 3), (4, 5), (6, 7)]
    inner = lax.ppermute(jnp.where(even, low, high), ROW, pairs + [(b, a) for a, b in pairs])
    above, below = jnp.where(even, outer, inner), jnp.where(even, inner, outer)
    corners = [part for row in (above, below) for part in (row[TC : TC + 1], row[TC + 1 :])]
    return (jnp.stack([above[:TC], below[:TC]]),) + sides(corners, west, east)


def whole_halo(tile, first, last):
    lower = lax.axis_index("c") == 0
    inner, outer = jnp.where(lower, last, first), jnp.where(lower, first, last)
    twin = lax.ppermute(inner, "c", [(0, 1), (1, 0)])
    chips = [(2 * k + 1, 2 * k + 2) for k in range(7)]
    chips = chips + [(b, a) for a, b in chips]
    chip = lax.ppermute(outer, COL, chips)
    rows, far = [], []
    for down, at in ((1, TR - 1), (-1, 0)):
        rows.append(shift(jnp.concatenate([tile[at], twin[at : at + 1]], axis=0), ROW, 8, down))
        pairs = [(16 * r + a, 16 * (r + down) + b) for r in range(8) for a, b in chips if 0 <= r + down < 8]
        far.append(lax.ppermute(outer[at : at + 1], ROW + COL, pairs))
    west, east = jnp.where(lower, chip, twin), jnp.where(lower, twin, chip)
    corners = []
    for row, cell in zip(rows, far):
        near = row[TC:]
        corners += [jnp.where(lower, cell, near), jnp.where(lower, near, cell)]
    return (jnp.stack([row[:TC] for row in rows]),) + sides(corners, west, east)


def local(coarse_in, fine_in, band_weight, point_weight, proj_weight, conv_weight, out_cot):
    core = lax.axis_index("c").astype(jnp.int32).reshape(1)
    swap = [(0, 1), (1, 0)]

    chunks = coarse_in.reshape(2, 8, 16, C).transpose(1, 0, 2, 3)
    west, east = side_edges(out_cot[:, 0], out_cot[:, TC - 1])
    chunks, west, east = lax.optimization_barrier((chunks, west, east))
    cot_halo = row_halo(out_cot, west, east)
    x = lax.all_to_all(chunks, ("xh", "y"), 0, 0, tiled=True).reshape(CELLS, C)
    dco = dcoarse_pass(out_cot, *cot_halo, conv_weight)
    x, dco = lax.optimization_barrier((x, dco))
    xtwin, dtwin = lax.ppermute(x, "c", swap), lax.ppermute(dco, "c", swap)
    packed, conv_in, edges, keep, send = forward_pass(
        core, x, xtwin, band_weight, point_weight, proj_weight, fine_in, out_cot, dco, dtwin, *cot_halo
    )
    got = lax.ppermute(send, "c", swap)
    late = (keep.astype(F32) + got.astype(F32)).astype(BF)
    packed = lax.dynamic_update_slice(packed, late, (0, 0))

    packed, conv_in, edges = lax.optimization_barrier((packed, conv_in, edges))
    parts = lax.all_to_all(packed, CHIPS, 0, 0, tiled=True)
    conv_halo = whole_halo(conv_in, edges[0], edges[1])
    spread = reduce_pass(parts)
    spread, conv_halo = lax.optimization_barrier((spread, conv_halo))
    mine = lax.all_to_all(spread, CHIPS, 0, 0, tiled=True)
    fine_out = conv_pass(conv_in, *conv_halo, conv_weight)
    mine, fine_out = lax.optimization_barrier((mine, fine_out))
    other = lax.ppermute(mine, "c", swap)
    grads = place_half(core, mine)
    grad_conv, grad_band, grad_point, grad_proj = place_half(1 - core, other, grads)
    return fine_out, grad_conv, grad_band, grad_point, grad_proj


def solution(mesh):
    fine_mesh = Mesh(
        np.asarray(mesh.devices).reshape([n for _, n in GRID]), tuple(name for name, _ in GRID)
    )
    fine = P(ROW, COL, None)
    in_specs = (P(ROW + COL, None, None), fine, P(), P(), P(), P(), fine)
    out_specs = (fine, P(), P(), P(), P())
    return jax.shard_map(local, mesh=fine_mesh, in_specs=in_specs, out_specs=out_specs, check_vma=False)
```

```python
import functools

import jax
import jax.numpy as jnp
import numpy as np
from jax import lax
from jax.experimental import pallas as pl
from jax.experimental.pallas import tpu as pltpu
from jax.sharding import Mesh
from jax.sharding import PartitionSpec as P

BF = jnp.bfloat16
F32 = jnp.float32
ROW = ("xl", "z")
COL = ("xh", "y", "c")
CHIPS = ("xl", "z", "xh", "y")
GRID = (("xl", 2), ("z", 4), ("xh", 2), ("y", 4), ("c", 2))

C, CF, BANDS, TAPS = 512, 256, 4, 9
TR, TC = 128, 32
IR, IC = 32, 8
CELLS = IR * IC
PAIR = 2 * CELLS
HB = 32
NB = TR // HB
SIDE = 136
LATE = TAPS * 2 * 128 + 256
EARLY = 5 * 4 * 256 + 2 * 256
PACK = LATE + EARLY
PEERS = 64
SCALE = float(1024 * 512) ** (-0.5)
MIB = 1024 * 1024
GELU_A = 0.7978845608028654
GELU_B = 0.044715


def params(mib, grid=1):
    return pltpu.CompilerParams(
        vmem_limit_bytes=mib * MIB, dimension_semantics=("arbitrary",) * grid if grid else None
    )


def cost(flops, moved):
    return pl.CostEstimate(flops=flops, bytes_accessed=moved, transcendentals=0)


def whole(*shape):
    return pl.BlockSpec(shape, lambda i: (0,) * len(shape))


def dot(a, b, dims=((1,), (0,))):
    return lax.dot_general(a, b, (dims, ((), ())), preferred_element_type=F32)


def iotas(*shape):
    return tuple(lax.broadcasted_iota(jnp.int32, shape, n) for n in range(len(shape)))


def haar_matrix():
    row, col = iotas(256, 256)
    inside = ((row >> 3) & 7 == col >> 5) & (row & 7 == (col & 15) >> 1)
    flip = ((row >> 6) & col & 1) ^ ((row >> 7) & (col >> 4) & 1)
    return jnp.where(inside, 0.5 - flip.astype(F32), 0.0).astype(BF)


def pool_matrix():
    row, col = iotas(TAPS * IC, 6 * TC)
    tap, j = row >> 3, row & 7
    a = (tap >= 3).astype(jnp.int32) + (tap >= 6).astype(jnp.int32)
    u = (col >> 5) + a - 2
    v = (col & 31) + (tap - 3 * a) - 1 - 4 * j
    return ((u >= 0) & (u < 4) & (v >= 0) & (v < 4)).astype(F32).astype(BF)


def side_matrix():
    row, col = iotas(3 * IR, SIDE)
    u = col + (row >> 5) - 2 - 4 * (row & 31)
    return ((u >= 0) & (u < 4)).astype(F32).astype(BF)


def dcoarse_kernel(oc, rows, left, right, wconv, out, pooled):
    pool, side = pool_matrix(), side_matrix()
    for i in range(IR):
        if i == 0:
            block = jnp.concatenate([rows[0], oc[: 5 * TC, :]], axis=0)
        elif i == IR - 1:
            block = jnp.concatenate([oc[(4 * i - 1) * TC :, :], rows[1]], axis=0)
        else:
            block = oc[(4 * i - 1) * TC : (4 * i + 5) * TC, :]
        part = dot(pool, block)
        for t in range(TAPS):
            for h in range(2):
                pooled[t, h, i * IC : (i + 1) * IC, :] = part[t * IC : (t + 1) * IC, h * 128 : (h + 1) * 128]
    for edge, b, start in ((left, 2, 0), (right, 0, IC - 1)):
        part = dot(side, edge[...].astype(BF))
        for a in range(3):
            for h in range(2):
                cells = pl.ds(start, IR, stride=IC)
                pooled[3 * a + b, h, cells, :] += part[a * IR : (a + 1) * IR, h * 128 : (h + 1) * 128]
    total = jnp.zeros((CELLS, CF), F32)
    for t in range(TAPS):
        s = jnp.concatenate([pooled[t, 0], pooled[t, 1]], axis=-1).astype(BF)
        total += dot(s, wconv[t], ((1,), (1,)))
    out[...] = total.astype(BF)


def dcoarse_pass(oc, rows, left, right, wconv):
    vm = pl.BlockSpec(memory_space=pltpu.VMEM)
    return pl.pallas_call(
        dcoarse_kernel,
        in_specs=[vm] * 5,
        out_specs=vm,
        out_shape=jax.ShapeDtypeStruct((CELLS, CF), BF),
        scratch_shapes=[pltpu.VMEM((TAPS, 2, CELLS, 128), F32)],
        compiler_params=params(16, 0),
        cost_estimate=cost(1_000, 1_000),
        name="coarse_cotangent",
    )(oc.reshape(TR * TC, CF), rows, left, right, wconv)


def coarse_gradients(core, haar, x, wproj, sub, slope, hidden, dco, dtwin, out, both):
    own = pl.multiple_of(core[0] * IC, IC)
    both[:, :, :, pl.ds(own, IC), :] = dco[...].astype(F32).reshape(8, 2, 2, IC, CF)
    both[:, :, :, pl.ds(IC - own, IC), :] = dtwin[...].astype(F32).reshape(8, 2, 2, IC, CF)
    d = jnp.concatenate([both[:, g].reshape(CELLS, CF) for g in range(2)], axis=0).astype(BF)
    dpre = (dot(d, wproj[...], ((1,), (1,))) * slope[...]).astype(BF)
    dmix = [dot(haar, dpre[g * 256 : (g + 1) * 256]).astype(BF) for g in range(2)]
    half = pl.ds(pl.multiple_of(core[0] * 256, 256), 256)
    for k in range(5):
        if k < BANDS:
            dk = jnp.concatenate([dmix[g][k * 64 : (k + 1) * 64] for g in range(2)], axis=0)
            grad = dot(sub[k * 128 : (k + 1) * 128, half], dk, ((0,), (0,)))
        else:
            grad = dot(x[:, half], dpre, ((0,), (0,)))
        for n in range(4):
            out[(4 * k + n) * 256 : (4 * k + n + 1) * 256, :] = grad[:, n * 128 : (n + 1) * 128].astype(BF)
    grad = dot(hidden[:, half], d, ((0,), (0,)))
    for n in range(2):
        out[(20 + n) * 256 : (21 + n) * 256, :] = grad[:, n * 128 : (n + 1) * 128].astype(BF)


def forward_kernel(
    core, x_hbm, xtwin_hbm, wb_hbm, wp_hbm, wj_hbm, fine_hbm, oc_hbm, dco, dtwin, rows, left, right,
    packed, conv_in, edges, keep, send,
    x, wband, wpoint, wproj, fine, oc, split, outs, up, ends, win, shifted, acc,
    sub, slope, hidden, early, both, sems,
):
    at = pl.multiple_of(core[0] * CELLS, CELLS)
    pairs = [(x_hbm, x.at[pl.ds(at, CELLS)])] + [(wb_hbm.at[k], wband.at[k]) for k in range(BANDS)]
    pairs += [(wp_hbm, wpoint), (wj_hbm, wproj), (fine_hbm, fine), (oc_hbm, oc)]
    pairs += [(xtwin_hbm, x.at[pl.ds(CELLS - at, CELLS)])]
    loads = [pltpu.make_async_copy(src, dst, sems.at[n]) for n, (src, dst) in enumerate(pairs)]
    store = pltpu.make_async_copy(early, packed.at[pl.ds(LATE, EARLY)], sems.at[len(pairs)])

    for load in loads[:1] + loads[-1:] + loads[1:-1]:
        load.start()
    haar = haar_matrix()
    loads[0].wait()
    loads[-1].wait()
    parts = [dot(haar, x[g * 256 : (g + 1) * 256, :]).astype(BF) for g in range(2)]
    for k in range(BANDS):
        part = jnp.concatenate([p[k * 64 : (k + 1) * 64] for p in parts], axis=0)
        sub[k * 128 : (k + 1) * 128, :] = part
        loads[1 + k].wait()
        m = dot(part, wband[k])
        hi = m.astype(BF)
        lo = (m - hi.astype(F32)).astype(BF)
        for g in range(2):
            split[g, 0, k * 64 : (k + 1) * 64, :] = hi[g * 64 : (g + 1) * 64]
            split[g, 1, k * 64 : (k + 1) * 64, :] = lo[g * 64 : (g + 1) * 64]
    loads[5].wait()
    loads[6].wait()
    for g in range(2):
        cells = slice(g * 256, (g + 1) * 256)
        value = dot(haar, split[g, 0], ((0,), (0,))) + dot(haar, split[g, 1], ((0,), (0,)))
        value = value + dot(x[cells, :], wpoint[...])
        square = value * value
        th = jnp.tanh(GELU_A * (value + GELU_B * (value * square)))
        slope[cells, :] = 0.5 * (1.0 + th) + 0.5 * value * (1.0 - th * th) * (GELU_A * (1.0 + 3.0 * GELU_B * square))
        act = (0.5 * value * (1.0 + th)).astype(BF)
        hidden[cells, :] = act
        outs[:, g] = dot(act, wproj[...]).astype(BF).astype(F32).reshape(8, 2, 16, CF)
    coarse_gradients(core, haar, x, wproj, sub, slope, hidden, dco, dtwin, early, both)
    store.start()
    loads[7].wait()
    loads[8].wait()

    def prepare(i):
        r0, slot = i * HB, i % 2
        for q in range(HB // 4):
            at = r0 // 4 + q
            cell = outs[at // 4, at // 2 % 2, at % 2, own, :]
            for s in range(4):
                up[slot, q, 0, pl.ds(s, IC, stride=4), :] = cell[:, :128]
                up[slot, q, 1, pl.ds(s, IC, stride=4), :] = cell[:, 128:]
            grown = jnp.concatenate([up[slot, q, 0], up[slot, q, 1]], axis=-1)
            for t in range(4):
                r = r0 + 4 * q + t
                value = fine[r].astype(F32) + grown
                fine[r] = value.astype(BF)
                ends[0, r : r + 1, :] = value[:1]
                ends[1, r : r + 1, :] = value[TC - 1 :]
        before = rows[0:1] if i == 0 else oc[r0 - 1 : r0]
        after = rows[1:2] if i == NB - 1 else oc[r0 + HB : r0 + HB + 1]
        fill_windows(r0, before, oc[r0 : r0 + HB], after, left, right, win.at[slot])
        for b in range(3):
            shifted[slot, :, :, b * CF : (b + 1) * CF] = win[slot, :, 9 - b : 9 - b + TC, :].astype(BF)

    def multiply(i):
        cells = fine[i * HB : (i + 1) * HB].reshape(HB * TC, CF).T
        for a in range(3):
            part = dot(cells, shifted[i % 2, 2 - a : 2 - a + HB].reshape(HB * TC, 3 * CF))
            acc[a] = part if i == 0 else acc[a] + part

    own = pl.ds(pl.multiple_of(core[0] * IC, IC), IC)
    prepare(0)
    for i in range(NB):
        if i + 1 < NB:
            prepare(i + 1)
        multiply(i)
    back = pltpu.make_async_copy(fine, conv_in, sems.at[len(pairs) + 1])
    back.start()
    edges[...] = ends[...].astype(BF)
    for out, c in ((keep, core[0]), (send, 1 - core[0])):
        half = pl.ds(pl.multiple_of(c * 128, 128), 128)
        for t in range(TAPS):
            for n in range(2):
                at = (t % 3) * CF + n * 128
                out[(2 * t + n) * 128 : (2 * t + n + 1) * 128, :] = acc[t // 3, half, at : at + 128].astype(BF)
        out[TAPS * 256 :, :] = jnp.zeros((LATE - TAPS * 256, 128), BF)
    store.wait()
    back.wait()


def forward_pass(core, x, xtwin, wband, wpoint, wproj, fine, oc, dco, dtwin, rows, left, right):
    hbm, vm = pl.BlockSpec(memory_space=pltpu.HBM), pl.BlockSpec(memory_space=pltpu.VMEM)
    return pl.pallas_call(
        forward_kernel,
        in_specs=[pl.BlockSpec(memory_space=pltpu.SMEM)]
        + [hbm] * 7
        + [vm] * 5,
        out_specs=[hbm, hbm, vm, vm, vm],
        out_shape=[
            jax.ShapeDtypeStruct((PACK, 128), BF),
            jax.ShapeDtypeStruct((TR, TC, CF), BF),
            jax.ShapeDtypeStruct((2, TR, CF), BF),
            jax.ShapeDtypeStruct((LATE, 128), BF),
            jax.ShapeDtypeStruct((LATE, 128), BF),
        ],
        scratch_shapes=[
            pltpu.VMEM((PAIR, C), BF),
            pltpu.VMEM((BANDS, C, C), BF),
            pltpu.VMEM((C, C), BF),
            pltpu.VMEM((C, CF), BF),
            pltpu.VMEM((TR, TC, CF), BF),
            pltpu.VMEM((TR, TC, CF), BF),
            pltpu.VMEM((2, 2, 256, C), BF),
            pltpu.VMEM((8, 2, 2, 2 * IC, CF), F32),
            pltpu.VMEM((2, HB // 4, 2, TC, 128), F32),
            pltpu.VMEM((2, TR, CF), F32),
            pltpu.VMEM((2, HB + 2, 48, CF), F32),
            pltpu.VMEM((2, HB + 2, TC, 3 * CF), BF),
            pltpu.VMEM((3, CF, 3 * CF), F32),
            pltpu.VMEM((PAIR, C), BF),
            pltpu.VMEM((PAIR, C), F32),
            pltpu.VMEM((PAIR, C), BF),
            pltpu.VMEM((EARLY, 128), BF),
            pltpu.VMEM((8, 2, 2, 2 * IC, CF), F32),
            pltpu.SemaphoreType.DMA((12,)),
        ],
        compiler_params=params(50, 0),
        cost_estimate=cost(8_000_000_000, 14_000_000),
        name="forward_and_gradients",
    )(core, x, xtwin, wband, wpoint, wproj, fine, oc, dco, dtwin, rows, left, right)


def window_specs():
    return [
        pl.BlockSpec((1, TC, CF), lambda i: (jnp.maximum(i * HB - 1, 0), 0, 0)),
        pl.BlockSpec((HB, TC, CF), lambda i: (i, 0, 0)),
        pl.BlockSpec((1, TC, CF), lambda i: (jnp.minimum(i * HB + HB, TR - 1), 0, 0)),
        whole(2, TC, CF),
        whole(SIDE, CF),
        whole(SIDE, CF),
    ]


def fill_windows(r0, before, tile, after, left, right, win):
    win[1 : HB + 1, 8 : 8 + TC, :] = tile.astype(F32)
    win[0:1, 8 : 8 + TC, :] = before.astype(F32)
    win[HB + 1 : HB + 2, 8 : 8 + TC, :] = after.astype(F32)
    for r in range(HB + 2):
        win[r, 7:8, :] = left[pl.ds(r0 + r, 1), :]
        win[r, 8 + TC : 9 + TC, :] = right[pl.ds(r0 + r, 1), :]


def conv_kernel(before, ci, after, rows, left, right, wconv, out, win, wide):
    i = pl.program_id(0)
    above = jnp.where(i == 0, rows[0:1], before[...])
    below = jnp.where(i == NB - 1, rows[1:2], after[...])
    fill_windows(i * HB, above, ci[...], below, left, right, win)
    for b in range(3):
        wide[:, :, b * CF : (b + 1) * CF] = win[:, 7 + b : 7 + b + TC, :].astype(BF)
    total = jnp.zeros((HB * TC, CF), F32)
    for a in range(3):
        total += dot(wide[a : a + HB].reshape(HB * TC, 3 * CF), wconv[a])
    out[...] = total.astype(BF).reshape(HB, TC, CF)


def conv_pass(ci, rows, left, right, wconv):
    return pl.pallas_call(
        conv_kernel,
        grid=(NB,),
        in_specs=window_specs() + [whole(3, 3 * CF, CF)],
        out_specs=pl.BlockSpec((HB, TC, CF), lambda i: (i, 0, 0)),
        out_shape=jax.ShapeDtypeStruct((TR, TC, CF), BF),
        scratch_shapes=[pltpu.VMEM((HB + 2, 48, CF), F32), pltpu.VMEM((HB + 2, TC, 3 * CF), BF)],
        compiler_params=params(16),
        cost_estimate=cost(1_000_000, 1_000_000),
        name="conv_forward",
    )(ci, ci, ci, rows, left, right, wconv.reshape(3, 3 * CF, CF))


def reduce_kernel(parts, out, held, copies, sems):
    n, m = held.shape[2], copies.shape[1]
    loads, stores = [], []
    for q in range(4):
        rows = pl.ds(q * n, n)
        loads.append(pltpu.make_async_copy(parts.at[:, rows], held.at[q], sems.at[q]))
        for g in range(PEERS // m):
            place = out.at[pl.ds(g * m, m), rows]
            stores.append(pltpu.make_async_copy(copies.at[q], place, sems.at[4 + len(stores)]))
    for load in loads:
        load.start()
    for q in range(4):
        loads[q].wait()
        done = (jnp.sum(held[q].astype(F32), axis=0) * SCALE).astype(BF)
        for p in range(m):
            copies[q, p] = done
        for store in stores[q * (PEERS // m) : (q + 1) * (PEERS // m)]:
            store.start()
    for store in stores:
        store.wait()


def reduce_pass(parts):
    n = PACK // PEERS
    hbm = pl.BlockSpec(memory_space=pltpu.HBM)
    return pl.pallas_call(
        reduce_kernel,
        in_specs=[hbm],
        out_specs=hbm,
        out_shape=jax.ShapeDtypeStruct((PEERS, n, 128), BF),
        scratch_shapes=[
            pltpu.VMEM((4, PEERS, n // 4, 128), BF),
            pltpu.VMEM((4, 16, n // 4, 128), BF),
            pltpu.SemaphoreType.DMA((20,)),
        ],
        compiler_params=params(56, 0),
        name="chip_sum",
    )(parts.reshape(PEERS, n, 128)).reshape(PACK, 128)


def place_kernel(core, half, *refs):
    conv, band, point, proj, conv_s, band_s, point_s, proj_s, sems = refs[-9:]
    large = pl.ds(pl.multiple_of(core[0] * 256, 256), 256)
    small = pl.ds(pl.multiple_of(core[0] * 128, 128), 128)
    groups = [(LATE + 1024 * k, 256, [band_s.at[k]], band_s.at[k], band.at[k, large]) for k in range(BANDS)]
    groups.append((LATE + 4096, 256, [point_s], point_s, point.at[large]))
    groups.append((LATE + 5120, 256, [proj_s], proj_s, proj.at[large]))
    groups.append((0, 128, [conv_s.at[t] for t in range(TAPS)], conv_s, conv.at[:, small]))
    stores = []
    for g, (start, n, tiles, held, out) in enumerate(groups):
        for tile in tiles:
            for col in range(0, tile.shape[1], 128):
                tile[:, col : col + 128] = half[start : start + n, :].astype(F32)
                start += n
        stores.append(pltpu.make_async_copy(held, out, sems.at[g]))
        stores[g].start()
    for store in stores:
        store.wait()


def place_half(core, half, before=()):
    hbm, vm = pl.BlockSpec(memory_space=pltpu.HBM), pl.BlockSpec(memory_space=pltpu.VMEM)
    return pl.pallas_call(
        place_kernel,
        in_specs=[pl.BlockSpec(memory_space=pltpu.SMEM), vm] + [hbm] * len(before),
        out_specs=[hbm] * 4,
        out_shape=[
            jax.ShapeDtypeStruct((TAPS, CF, CF), F32),
            jax.ShapeDtypeStruct((BANDS, C, C), F32),
            jax.ShapeDtypeStruct((C, C), F32),
            jax.ShapeDtypeStruct((C, CF), F32),
        ],
        input_output_aliases={2 + n: n for n in range(len(before))},
        scratch_shapes=[
            pltpu.VMEM((TAPS, 128, CF), F32),
            pltpu.VMEM((BANDS, 256, C), F32),
            pltpu.VMEM((256, C), F32),
            pltpu.VMEM((256, CF), F32),
            pltpu.SemaphoreType.DMA((7,)),
        ],
        compiler_params=params(16, 0),
        cost_estimate=cost(0, 6_000_000),
        name="place_gradients",
    )(core, half, *before)


def shift(value, axes, count, step):
    pairs = [(i, i + step) for i in range(count) if 0 <= i + step < count]
    return lax.ppermute(value, axes, pairs)


def side_edges(first, last):
    lower = lax.axis_index("c") == 0
    twin = lax.ppermute(jnp.where(lower, last, first), "c", [(0, 1), (1, 0)])
    pairs = [(2 * k + 1, 2 * k + 2) for k in range(7)]
    pairs = pairs + [(b, a) for a, b in pairs]
    chip = lax.ppermute(jnp.where(lower, first, last), COL, pairs)
    return jnp.where(lower, chip, twin), jnp.where(lower, twin, chip)


def sides(corners, west, east):
    pad = jnp.zeros((SIDE - TR - 2, CF), BF)
    left = jnp.concatenate([corners[0], west, corners[2], pad], axis=0)
    right = jnp.concatenate([corners[1], east, corners[3], pad], axis=0)
    return left.astype(F32), right.astype(F32)


def row_halo(tile, west, east):
    low = jnp.concatenate([tile[TR - 1], west[TR - 1 :], east[TR - 1 :]], axis=0)
    high = jnp.concatenate([tile[0], west[:1], east[:1]], axis=0)
    even = lax.axis_index(ROW) % 2 == 0
    pairs = [(1, 2), (3, 4), (5, 6)]
    outer = lax.ppermute(jnp.where(even, high, low), ROW, pairs + [(b, a) for a, b in pairs])
    pairs = [(0, 1), (2, 3), (4, 5), (6, 7)]
    inner = lax.ppermute(jnp.where(even, low, high), ROW, pairs + [(b, a) for a, b in pairs])
    above, below = jnp.where(even, outer, inner), jnp.where(even, inner, outer)
    corners = [part for row in (above, below) for part in (row[TC : TC + 1], row[TC + 1 :])]
    return (jnp.stack([above[:TC], below[:TC]]),) + sides(corners, west, east)


def whole_halo(tile, first, last):
    lower = lax.axis_index("c") == 0
    inner, outer = jnp.where(lower, last, first), jnp.where(lower, first, last)
    twin = lax.ppermute(inner, "c", [(0, 1), (1, 0)])
    chips = [(2 * k + 1, 2 * k + 2) for k in range(7)]
    chips = chips + [(b, a) for a, b in chips]
    chip = lax.ppermute(outer, COL, chips)
    rows, far = [], []
    for down, at in ((1, TR - 1), (-1, 0)):
        rows.append(shift(jnp.concatenate([tile[at], twin[at : at + 1]], axis=0), ROW, 8, down))
        pairs = [(16 * r + a, 16 * (r + down) + b) for r in range(8) for a, b in chips if 0 <= r + down < 8]
        far.append(lax.ppermute(outer[at : at + 1], ROW + COL, pairs))
    west, east = jnp.where(lower, chip, twin), jnp.where(lower, twin, chip)
    corners = []
    for row, cell in zip(rows, far):
        near = row[TC:]
        corners += [jnp.where(lower, cell, near), jnp.where(lower, near, cell)]
    return (jnp.stack([row[:TC] for row in rows]),) + sides(corners, west, east)


def local(coarse_in, fine_in, band_weight, point_weight, proj_weight, conv_weight, out_cot):
    core = lax.axis_index("c").astype(jnp.int32).reshape(1)
    swap = [(0, 1), (1, 0)]

    chunks = coarse_in.reshape(2, 8, 16, C).transpose(1, 0, 2, 3)
    west, east = side_edges(out_cot[:, 0], out_cot[:, TC - 1])
    chunks, west, east = lax.optimization_barrier((chunks, west, east))
    cot_halo = row_halo(out_cot, west, east)
    x = lax.all_to_all(chunks, ("xh", "y"), 0, 0, tiled=True).reshape(CELLS, C)
    dco = dcoarse_pass(out_cot, *cot_halo, conv_weight)
    x, dco = lax.optimization_barrier((x, dco))
    xtwin, dtwin = lax.ppermute(x, "c", swap), lax.ppermute(dco, "c", swap)
    packed, conv_in, edges, keep, send = forward_pass(
        core, x, xtwin, band_weight, point_weight, proj_weight, fine_in, out_cot, dco, dtwin, *cot_halo
    )
    got = lax.ppermute(send, "c", swap)
    late = (keep.astype(F32) + got.astype(F32)).astype(BF)
    packed = lax.dynamic_update_slice(packed, late, (0, 0))

    packed, conv_in, edges = lax.optimization_barrier((packed, conv_in, edges))
    parts = lax.all_to_all(packed, CHIPS, 0, 0, tiled=True)
    conv_halo = whole_halo(conv_in, edges[0], edges[1])
    spread = reduce_pass(parts)
    spread, conv_halo = lax.optimization_barrier((spread, conv_halo))
    mine = lax.all_to_all(spread, CHIPS, 0, 0, tiled=True)
    fine_out = conv_pass(conv_in, *conv_halo, conv_weight)
    mine, fine_out = lax.optimization_barrier((mine, fine_out))
    other = lax.ppermute(mine, "c", swap)
    grads = place_half(core, mine)
    grad_conv, grad_band, grad_point, grad_proj = place_half(1 - core, other, grads)
    return fine_out, grad_conv, grad_band, grad_point, grad_proj


def solution(mesh):
    fine_mesh = Mesh(
        np.asarray(mesh.devices).reshape([n for _, n in GRID]), tuple(name for name, _ in GRID)
    )
    fine = P(ROW, COL, None)
    in_specs = (P(ROW + COL, None, None), fine, P(), P(), P(), P(), fine)
    out_specs = (fine, P(), P(), P(), P())
    return jax.shard_map(local, mesh=fine_mesh, in_specs=in_specs, out_specs=out_specs, check_vma=False)
```
